256 devices in a mesh: node: 16 (over y_hi, x, core), replica: 16 (over y_lo, z).
Axes of the slice: x: 4, y: 4 (y_hi: 2, y_lo: 2; y = y_hi * 2 + y_lo), z: 8, core: 2. Of those that a mesh axis runs over, the one named last changes fastest.
Arguments:
- hidden_act: bfloat16 [196608, 1024], P(('node', 'replica')), may hold values from -24 to 24
- out_grad: bfloat16 [196608, 3584], P(('node', 'replica')), may hold values from -0.023925781 to 0.023925781
- tile_list: int32 [16, 16, 2, 6], P('node', 'replica'), may hold values from 0 to 5, as said below
- tile_count: int32 [16, 16, 2], P('node', 'replica'), may hold values from 1 to 5, as said below
- momentum: float32 [2, 1024, 3584], P(None, 'node'), may hold values from -6 to 6
- weight: bfloat16 [2, 1024, 3584], P(None, 'node'), may hold values from -0.1875 to 0.1875
- next_act: bfloat16 [2, 16384, 1024], P(None, ('node', 'replica')), may hold values from -6 to 6
Outputs:
- new_momentum: float32 [2, 1024, 3584], P(None, 'node')
- next_out: bfloat16 [2, 16384, 3584], P(None, ('node', 'replica'))
The draws below stay inside these ranges and needn't reach their ends.
Inputs may be any that keep to these rules, and one draw needn't show every extreme that they name: `tile_list`: for each device and expert the first tile_count entries name distinct tiles of that device; the two experts' named tiles together cover every tile of the device exactly once; entries past the count are tile numbers without meaning. `tile_count`: the counts of one device sum to 6.
All inputs are finite; a program needn't handle non-finite values.
Results may differ from the reference program's by a relative error of at most 0.022.
Values may be sent and summed in bfloat16 or wider, within the bound.
No kernel may reach another device: no remote copies, remote signals or barrier semaphores. Data moves between devices by JAX's collectives and lax.ppermute only.
A program may use at most 128 MiB of HBM per device.

```python
import jax
import jax.numpy as jnp
from jax import lax

H = 1024
D = 3584
TILE = 128
BUCKETS = 2
TILES_DEV = 6
NODES = 16
REPLICAS = 16
ROWS = 196608
NEXT_TOTAL = 16384
N_NODE = 16
N_REPLICA = 16


def tile_routes(key):
    device_total = NODES * REPLICAS
    order_keys = jax.random.split(jax.random.fold_in(key, 11), device_total)
    orders = jax.vmap(lambda single: jax.random.permutation(single, TILES_DEV))(order_keys).astype(jnp.int32)
    first_count = jax.random.randint(jax.random.fold_in(key, 12), (device_total,), 1, TILES_DEV).astype(jnp.int32)
    first_count = first_count.at[0].set(TILES_DEV - 1).at[1].set(1)
    second_count = TILES_DEV - first_count
    shifted = (jnp.arange(TILES_DEV, dtype=jnp.int32)[None, :] + first_count[:, None]) % TILES_DEV
    rolled = jnp.take_along_axis(orders, shifted, axis=1)
    route_lists = jnp.stack([orders, rolled], axis=1).reshape(NODES, REPLICAS, 2, TILES_DEV)
    route_counts = jnp.stack([first_count, second_count], axis=1).reshape(NODES, REPLICAS, 2)
    return (route_lists, route_counts)


def draw_tile_list(key, part):
    return tile_routes(key)[0]


def draw_tile_count(key, part):
    return tile_routes(key)[1]


def with_spikes(array, own_key, source, target, shards_of, factor):
    def block_of(axis_at):
        return (jnp.arange(array.shape[axis_at]) // (array.shape[axis_at] // shards_of)).reshape((-1,) + (1,) * (array.ndim - 1 - axis_at))

    near = jax.random.permutation(own_key, shards_of)[block_of(target)]
    far = (block_of(target) + shards_of // 2) % shards_of
    return jnp.where((block_of(source) == near) | (block_of(source) == far), factor * array, array)


def shard_levels(rng, dims, cuts, least, top_value):
    level = 1.0
    for dim, shards_of in cuts:
        draws = jax.random.uniform(jax.random.fold_in(jax.random.fold_in(rng, 6), dim), (shards_of,), jnp.float32, least / len(cuts), top_value / len(cuts))
        level = level * jnp.repeat(jnp.exp(draws), dims[dim] // shards_of).reshape((-1,) + (1,) * (len(dims) - 1 - dim))
    return level


def normal_values(rng, dims, deviation, limit, shards=(), kind=jnp.bfloat16):
    entries = deviation * jax.random.normal(rng, dims, jnp.float32)
    if shards:
        entries = entries * shard_levels(rng, dims, shards, -0.22, 0.18)
    return jnp.clip(entries, -limit, limit).astype(kind)


def bell_draw_with(own_key, dims, width, limit, shards, heavy, held_as=jnp.bfloat16):
    values = width * jax.random.normal(own_key, dims, jnp.float32)
    if shards:
        values = values * shard_levels(own_key, dims, shards, -0.22, 0.18)
    return jnp.clip(with_spikes(values, jax.random.fold_in(own_key, 3), *heavy), -limit, limit).astype(held_as)


def setup_inputs(seed: int = 0) -> dict:
    seeds = jax.random.split(jax.random.key(seed), 8)
    return {
        "hidden_act": bell_draw_with(seeds[0], (ROWS, H), 1.0, 24.0, ((0, 256),), (0, 1, 256, 6.0)),
        "out_grad": normal_values(seeds[1], (ROWS, D), 0.004, 0.023925781, ((0, 256),)),
        "tile_list": draw_tile_list(jax.random.fold_in(seeds[7], 71), 0),
        "tile_count": draw_tile_count(jax.random.fold_in(seeds[7], 71), 0),
        "momentum": normal_values(seeds[4], (BUCKETS, H, D), 1.0, 6.0, ((1, 16),), jnp.float32),
        "weight": normal_values(seeds[5], (BUCKETS, H, D), H ** -0.5, 0.1875, ((1, 16),)),
        "next_act": normal_values(seeds[6], (BUCKETS, NEXT_TOTAL, H), 1.0, 6.0, ((1, 256),)),
    }


momentum_decay = 0.9
learning_rate = 0.01


def bucket_masks(route_lists, route_counts, tile_rows):
    tile_total = route_lists.shape[-1]
    tile_slots = jnp.arange(tile_total, dtype=jnp.int32)
    live_slot = tile_slots[None, :] < route_counts[:, None]
    named_tile = (route_lists[:, :, None] == tile_slots[None, None, :]) & live_slot[:, :, None]
    owned_tile = jnp.any(named_tile, axis=1)
    return jnp.repeat(owned_tile, tile_rows, axis=1)


def reference(hidden_act, out_grad, tile_list, tile_count, momentum, weight, next_act):
    devices = N_NODE * N_REPLICA
    rows_dev = TILE * TILES_DEV
    act_blocks = hidden_act.reshape(devices, rows_dev, H)
    grad_blocks = out_grad.reshape(devices, rows_dev, D)
    route_lists = tile_list.reshape(devices, BUCKETS, TILES_DEV)
    route_counts = tile_count.reshape(devices, BUCKETS)

    def add_device(running_sum, inputs):
        act_rows, grad_rows, dev_lists, dev_counts = inputs
        owned_rows = bucket_masks(dev_lists, dev_counts, TILE)
        bucket_terms = []
        for bucket in range(BUCKETS):
            masked = jnp.where(owned_rows[bucket][:, None], grad_rows, jnp.zeros_like(grad_rows))
            partial_grad = lax.dot_general(act_rows, masked, (((0,), (0,)), ((), ())), preferred_element_type=jnp.float32)
            rounded = lax.optimization_barrier(partial_grad.astype(jnp.bfloat16))
            bucket_terms.append(rounded.astype(jnp.float32))
        return running_sum + jnp.stack(bucket_terms), None

    zero_total = jnp.zeros((BUCKETS, H, D), jnp.float32)
    summed, unused = lax.scan(add_device, zero_total, (act_blocks, grad_blocks, route_lists, route_counts))
    new_momentum = momentum_decay * momentum + summed
    new_weight = (weight.astype(jnp.float32) - learning_rate * new_momentum).astype(jnp.bfloat16)
    next_out = jnp.einsum("bnh,bhd->bnd", next_act.astype(jnp.float32), new_weight.astype(jnp.float32))
    return new_momentum, next_out.astype(jnp.bfloat16)
```

```python
import functools

import jax
import jax.numpy as jnp
from jax import lax
from jax.experimental import pallas as pl
from jax.experimental.pallas import tpu as pltpu
from jax.sharding import PartitionSpec as P

BUCKETS = 2
TILE = 128
TILES = 6
AXES = ("node", "replica")
F32 = jnp.float32
BF16 = jnp.bfloat16

momentum_decay = 0.9
learning_rate = 0.01

NX, NZ = 4, 8
HALF = 1792
QUARTER = 896
ROUTE = BUCKETS * TILES + BUCKETS


def flat(yh, x, c, yl, z):
    return ((yh * NX + x) * 2 + c) * 16 + yl * NZ + z


def send(value, move):
    pairs = []
    for yh in range(2):
        for x in range(NX):
            for c in range(2):
                for yl in range(2):
                    for z in range(NZ):
                        here = flat(yh, x, c, yl, z)
                        pairs.append((here, flat(*move(yh, x, c, yl, z))))
    return lax.ppermute(value, AXES, pairs)


def shift_x(k):
    return lambda yh, x, c, yl, z: (yh, (x + k) % NX, c, yl, z)


def shift_y(k):
    def move(yh, x, c, yl, z):
        y = (yh * 2 + yl + k) % 4
        return y // 2, x, c, y % 2, z

    return move


def shift_z(k):
    return lambda yh, x, c, yl, z: (yh, x, c, yl, (z + k) % NZ)


def flip(dz, dc, dyl):
    return lambda yh, x, c, yl, z: (yh, x, c ^ dc, yl ^ dyl, z ^ dz)


def plane(dyh, k):
    return lambda yh, x, c, yl, z: (yh ^ dyh, (x + k) % NX, c, yl, z)


def vmem():
    return pl.BlockSpec(memory_space=pltpu.VMEM)


def smem():
    return pl.BlockSpec(memory_space=pltpu.SMEM)


def call(kernel, scalars, arrays, outs, scratch=(), flops=0, moved=0):
    return pl.pallas_call(
        kernel,
        out_shape=outs,
        in_specs=[smem()] + [vmem()] * len(arrays),
        out_specs=[vmem()] * len(outs),
        scratch_shapes=list(scratch),
        compiler_params=pltpu.CompilerParams(vmem_limit_bytes=48 * 1024 * 1024),
        cost_estimate=pl.CostEstimate(flops=flops, bytes_accessed=moved, transcendentals=0),
    )(scalars, *arrays)


def grad_kernel(offsets, s, hid_o, hid_t, og_o, og_t, *refs):
    acc_a, acc_b = refs[-2:]
    outs = list(refs[:-2])
    x, y, c = s[0], s[1], s[2]

    def tiles_dot(hid, og, route, pair, expert, lanes, first, width):
        count = s[route + BUCKETS * TILES + expert]
        t0 = s[route + expert * TILES + 2 * pair]
        t1 = s[route + expert * TILES + 2 * pair + 1]
        r0 = pl.ds(pl.multiple_of(t0 * TILE, TILE), TILE)
        r1 = pl.ds(pl.multiple_of(t1 * TILE, TILE), TILE)
        both = 2 * pair + 1 < count
        cols = pl.ds(pl.multiple_of(first, 128), width)
        parts = []
        for lane, span in lanes:
            at = pl.ds(pl.multiple_of(lane, 128), span)
            h0 = hid[r0, at]
            h1 = hid[r1, at]
            h1 = jnp.where(both, h1, jnp.zeros_like(h1))
            parts.append(jnp.concatenate([h0, h1], axis=0))
        left = parts[0] if len(parts) == 1 else jnp.concatenate(parts, axis=1)
        right = jnp.concatenate([og[r0, cols], og[r1, cols]], axis=0)
        return lax.dot_general(
            left, right, (((0,), (0,)), ((), ())), preferred_element_type=F32
        )

    def piece(acc, expert, lanes, first, width):
        own, other = 3, 3 + ROUTE
        acc[...] = tiles_dot(hid_o, og_o, own, 0, expert, lanes, c * HALF + first, width)

        def more(pair, carry):
            acc[...] += tiles_dot(hid_o, og_o, own, pair, expert, lanes, c * HALF + first, width)
            return carry

        def theirs(pair, carry):
            acc[...] += tiles_dot(hid_t, og_t, other, pair, expert, lanes, first, width)
            return carry

        n_own = (s[own + BUCKETS * TILES + expert] + 1) // 2
        n_other = (s[other + BUCKETS * TILES + expert] + 1) // 2
        lax.fori_loop(1, n_own, more, 0)
        lax.fori_loop(0, n_other, theirs, 0)

    def store(acc, k):
        if k == 0:
            outs.pop(0)[...] = acc[...].astype(BF16)
        else:
            half = acc.shape[0] // 2
            outs.pop(0)[...] = acc[:half].astype(BF16)
            outs.pop(0)[...] = acc[half:].astype(BF16)

    for k in offsets:
        xk = lax.rem(x + k, NX)
        piece(acc_a, 0, [(xk * 128, 128), ((xk + NX) * 128, 128)], 0, HALF)
        store(acc_a, k)
        yk = lax.rem(y + k, 4)
        piece(acc_b, 1, [((yk // 2) * 512, 512)], lax.rem(yk, 2) * QUARTER, QUARTER)
        store(acc_b, k)


def gradients(offsets, scalars, hid_o, hid_t, og_o, og_t):
    outs = []
    for k in offsets:
        if k == 0:
            shapes = [(256, HALF), (512, QUARTER)]
        else:
            shapes = [(128, HALF)] * 2 + [(256, QUARTER)] * 2
        outs += [jax.ShapeDtypeStruct(shape, BF16) for shape in shapes]
    scratch = [pltpu.VMEM((256, HALF), F32), pltpu.VMEM((512, QUARTER), F32)]
    made = call(
        functools.partial(grad_kernel, offsets),
        scalars,
        [hid_o, hid_t, og_o, og_t],
        outs,
        scratch,
        flops=len(offsets) * 2 * 1536 * 256 * HALF,
        moved=11 * 2**20,
    )
    pieces = {}
    for k in offsets:
        take = 1 if k == 0 else 2
        a, made = made[:take], made[take:]
        b, made = made[:take], made[take:]
        pieces[k] = (a, b)
    return pieces


def add32(*terms):
    total = terms[0].astype(F32)
    for term in terms[1:]:
        total = total + term.astype(F32)
    return total


def ring_scatter(pieces, which, shift):
    lo2, hi2 = pieces[2][which]
    lo1, hi1 = pieces[1][which]
    lo3, hi3 = pieces[3][which]
    (own,) = pieces[0][which]
    half = own.shape[0] // 2
    far_lo = send(lo2, shift(1))
    far_hi = send(hi2, shift(-1))
    from_left_hi = send(hi1, shift(1))
    from_right_lo = send(lo3, shift(-1))
    from_left_lo = send(add32(lo1, far_lo).astype(BF16), shift(1))
    from_right_hi = send(add32(hi3, far_hi).astype(BF16), shift(-1))
    lower = add32(own[:half], from_right_lo, from_left_lo)
    upper = add32(own[half:], from_left_hi, from_right_hi)
    return jnp.concatenate([lower.astype(BF16), upper.astype(BF16)], axis=0)


def weight_kernel(s, base, own, back2, back4, back6, out):
    group = s[0] // 2
    for k, grad in enumerate((own, back2, back4, back6)):
        rows = pl.ds(pl.multiple_of(lax.rem(group - k + 4, 4) * 32, 32), 32)
        out[rows, :] = (base[rows, :] - learning_rate * grad[...].astype(F32)).astype(BF16)


def share_kernel(s, *refs):
    z, c = s[0], s[1]
    mine, other = refs[NZ:]
    for k in range(NZ):
        source = lax.rem(z - k + NZ, NZ)
        expert = lax.rem(source, 2)
        group = source // 2
        rows = pl.ds(pl.multiple_of(lax.rem(group, 2) * 32, 32), 32)
        core = group // 2

        @pl.when(core == c)
        def _():
            mine[expert, rows, :] = refs[k][...]

        @pl.when(core != c)
        def _():
            other[expert, rows, :] = refs[k][...]


def momentum_kernel(s, momentum, p00, p01, p10, p11, out):
    c, yl = s[1], s[2]
    for dc, dyl, grad in ((0, 0, p00), (0, 1, p01), (1, 0, p10), (1, 1, p11)):
        quarter = (c ^ dc) * 2 + (yl ^ dyl)
        cols = pl.ds(pl.multiple_of(quarter * QUARTER, 128), QUARTER)
        for e in range(BUCKETS):
            out[e, :, cols] = momentum_decay * momentum[e, :, cols] + grad[e].astype(F32)


GROUP = [(dz, dc, dyl) for dz in range(2) for dc in range(2) for dyl in range(2)]
PLANE = [(dyh, k) for dyh in range(2) for k in range(NX)]


def product_kernel(s, *refs):
    acts, weights, outs = refs[:8], refs[8:16], refs[16:24]
    left, right = refs[24:]
    yh, x = s[3], s[4]
    for i, (dyh, k) in enumerate(PLANE):
        m = (yh ^ dyh) * NX + lax.rem(x - k + NX, NX)
        cols = pl.ds(pl.multiple_of(m * 128, 128), 128)
        right[i * 128 : (i + 1) * 128, :] = weights[i][...]
        for j in range(8):
            left[j * 64 : (j + 1) * 64, i * 128 : (i + 1) * 128] = acts[j][:, cols]
    for j in range(0, 8, 4):
        total = jnp.dot(left[j * 64 : (j + 4) * 64, :], right[...], preferred_element_type=F32)
        for i in range(4):
            outs[j + i][...] = total[i * 64 : (i + 1) * 64].astype(BF16)


def join_kernel(s, *refs):
    out = refs[8]
    z, c, yl = s[0], s[1], s[2]
    for (dz, dc, dyl), piece in zip(GROUP, refs[:8]):
        quarter = (c ^ dc) * 2 + (yl ^ dyl)
        cols = pl.ds(pl.multiple_of(quarter * QUARTER, 128), QUARTER)
        out[lax.rem(z, 2) ^ dz, :, cols] = piece[...]


def local(hidden_act, out_grad, tile_list, tile_count, momentum, weight, next_act):
    node = lax.axis_index("node")
    replica = lax.axis_index("replica")
    yh, x, c = node // 8, (node // 2) % 4, node % 2
    yl, z = replica // NZ, replica % NZ
    z0 = z % 2
    y = yh * 2 + yl
    place = jnp.stack([z, c, yl, yh, x]).astype(jnp.int32)

    core = flip(0, 1, 0)
    hid_t = send(hidden_act, core)
    og_t = send(lax.dynamic_slice_in_dim(out_grad, (1 - c) * HALF, HALF, 1), core)
    route = jnp.concatenate([tile_list.reshape(-1), tile_count.reshape(-1)])
    scalars = jnp.concatenate(
        [jnp.stack([x, y, c]).astype(jnp.int32), route, send(route, core)]
    )
    base_all = weight.astype(F32) - learning_rate * (momentum_decay * momentum)

    def base_part(which):
        at = (z0, 0, (which * 2 + yl) * QUARTER)
        return lax.dynamic_slice(base_all, at, (1, 64, QUARTER))[0]

    base_own = base_part(c)
    base_t = send(base_part(1 - c), core)
    base = jnp.where(
        c == 0,
        jnp.concatenate([base_own, base_t], axis=0),
        jnp.concatenate([base_t, base_own], axis=0),
    )
    act_same = lax.dynamic_index_in_dim(next_act, z0, 0, False)
    act_other = lax.dynamic_index_in_dim(next_act, 1 - z0, 0, False)
    acts = [act_same] + [
        send(act_other if dz else act_same, flip(dz, dc, dyl)) for dz, dc, dyl in GROUP[1:]
    ]

    pieces = gradients((2,), scalars, hidden_act, hid_t, out_grad, og_t)
    pieces |= gradients((1, 3), scalars, hidden_act, hid_t, out_grad, og_t)
    pieces |= gradients((0,), scalars, hidden_act, hid_t, out_grad, og_t)

    part_a = ring_scatter(pieces, 0, shift_x)
    part_b = ring_scatter(pieces, 1, shift_y)

    def cut_a(k):
        yk = (y + k) % 4
        return lax.dynamic_slice(part_a, ((yk // 2) * 128, (yk % 2) * QUARTER), (128, QUARTER))

    def cut_b(k):
        return lax.dynamic_slice(part_b, (((x + k) % NX) * 128, 0), (128, QUARTER))

    plane_a = add32(cut_a(0), *[send(cut_a(k), shift_y(k)) for k in (2, 1, 3)])
    plane_b = add32(cut_b(0), *[send(cut_b(k), shift_x(k)) for k in (2, 1, 3)])
    both = jnp.stack([plane_a.astype(BF16), plane_b.astype(BF16)])

    def cut_z(k):
        zk = (z + k) % NZ
        return lax.dynamic_slice(both, (zk % 2, (zk // 2) * 32, 0), (1, 32, QUARTER))[0]

    far_first = (4, 3, 5, 2, 6, 1, 7)
    grad = add32(cut_z(0), *[send(cut_z(k), shift_z(k)) for k in far_first]).astype(BF16)
    groups = {0: grad}
    for k in (4, 2, 6, 3, 5, 1, 7):
        groups[k] = send(grad, shift_z(k))

    (own_weight,) = call(
        weight_kernel,
        place,
        [base] + [groups[k] for k in (0, 2, 4, 6)],
        [jax.ShapeDtypeStruct((128, QUARTER), BF16)],
        moved=2**20,
    )
    weights = [own_weight] + [send(own_weight, plane(dyh, k)) for dyh, k in PLANE[1:]]

    mine, other = call(
        share_kernel,
        place,
        [groups[k] for k in range(NZ)],
        [jax.ShapeDtypeStruct((BUCKETS, 64, QUARTER), BF16)] * 2,
        moved=2**20,
    )
    shares = [
        mine,
        send(mine, flip(0, 0, 1)),
        send(other, flip(0, 1, 0)),
        send(other, flip(0, 1, 1)),
    ]

    outs = call(
        product_kernel,
        place,
        acts + weights,
        [jax.ShapeDtypeStruct((64, QUARTER), BF16)] * 8,
        [pltpu.VMEM((512, 1024), BF16), pltpu.VMEM((1024, QUARTER), BF16)],
        flops=2 * 512 * 1024 * QUARTER,
        moved=4 * 2**20,
    )
    parts = [outs[0]] + [send(outs[i], flip(*GROUP[i])) for i in range(1, 8)]
    (next_out,) = call(
        join_kernel,
        place,
        parts,
        [jax.ShapeDtypeStruct((BUCKETS, 64, 2 * HALF), BF16)],
        moved=2 * 2**20,
    )
    (new_momentum,) = call(
        momentum_kernel,
        place,
        [momentum] + shares,
        [jax.ShapeDtypeStruct((BUCKETS, 64, 2 * HALF), F32)],
        moved=5 * 2**20,
    )
    return new_momentum, next_out


def solution(mesh):
    in_specs = (
        P(("node", "replica"), None),
        P(("node", "replica"), None),
        P("node", "replica", None, None),
        P("node", "replica", None),
        P(None, "node", None),
        P(None, "node", None),
        P(None, ("node", "replica"), None),
    )
    out_specs = (P(None, "node", None), P(None, ("node", "replica"), None))
    return jax.shard_map(local, mesh=mesh, in_specs=in_specs, out_specs=out_specs, check_vma=False)
```

```python
import functools

import jax
import jax.numpy as jnp
from jax import lax
from jax.experimental import pallas as pl
from jax.experimental.pallas import tpu as pltpu
from jax.sharding import PartitionSpec as P

BUCKETS = 2
TILE = 128
TILES = 6
AXES = ("y_hi", "x", "core", "y_lo", "z_hi", "z_lo")
GROUP = ("core", "y_lo", "z_lo")
F32 = jnp.float32
BF16 = jnp.bfloat16

momentum_decay = 0.9
learning_rate = 0.01

NX, NZ = 4, 8
HALF = 1792
QUARTER = 896
ROUTE = BUCKETS * TILES + BUCKETS


def flat(yh, x, c, yl, z):
    return ((yh * NX + x) * 2 + c) * 16 + yl * NZ + z


def send(value, move):
    pairs = []
    for yh in range(2):
        for x in range(NX):
            for c in range(2):
                for yl in range(2):
                    for z in range(NZ):
                        here = flat(yh, x, c, yl, z)
                        pairs.append((here, flat(*move(yh, x, c, yl, z))))
    return lax.ppermute(value, AXES, pairs)


def shift_x(k):
    return lambda yh, x, c, yl, z: (yh, (x + k) % NX, c, yl, z)


def shift_y(k):
    def move(yh, x, c, yl, z):
        y = (yh * 2 + yl + k) % 4
        return y // 2, x, c, y % 2, z

    return move


def shift_z(k):
    return lambda yh, x, c, yl, z: (yh, x, c, yl, (z + k) % NZ)


def flip(dz, dc, dyl):
    return lambda yh, x, c, yl, z: (yh, x, c ^ dc, yl ^ dyl, z ^ dz)


def plane(dyh, k):
    return lambda yh, x, c, yl, z: (yh ^ dyh, (x + k) % NX, c, yl, z)


def vmem():
    return pl.BlockSpec(memory_space=pltpu.VMEM)


def smem():
    return pl.BlockSpec(memory_space=pltpu.SMEM)


def near(shape, dtype=BF16):
    return pltpu.VMEM(shape, dtype)


def held(value):
    return pltpu.with_memory_space_constraint(value, pltpu.VMEM)


def call(kernel, scalars, arrays, outs, scratch=(), flops=0, moved=0, limit=12):
    return pl.pallas_call(
        kernel,
        out_shape=outs,
        in_specs=[smem()] + [vmem()] * len(arrays),
        out_specs=[vmem()] * len(outs),
        scratch_shapes=list(scratch),
        compiler_params=pltpu.CompilerParams(vmem_limit_bytes=limit * 1024 * 1024),
        cost_estimate=pl.CostEstimate(flops=flops, bytes_accessed=moved, transcendentals=0),
    )(scalars, *arrays)


def tiles_dot(s, hid, og, route, pair, expert, lanes, first, width):
    count = s[route + BUCKETS * TILES + expert]
    t0 = s[route + expert * TILES + 2 * pair]
    t1 = s[route + expert * TILES + 2 * pair + 1]
    r0 = pl.ds(pl.multiple_of(t0 * TILE, TILE), TILE)
    r1 = pl.ds(pl.multiple_of(t1 * TILE, TILE), TILE)
    both = 2 * pair + 1 < count
    cols = pl.ds(pl.multiple_of(first, 128), width)
    parts = []
    for lane, span in lanes:
        at = pl.ds(pl.multiple_of(lane, 128), span)
        h0 = hid[r0, at]
        h1 = hid[r1, at]
        h1 = jnp.where(both, h1, jnp.zeros_like(h1))
        parts.append(jnp.concatenate([h0, h1], axis=0))
    left = parts[0] if len(parts) == 1 else jnp.concatenate(parts, axis=1)
    right = jnp.concatenate([og[r0, cols], og[r1, cols]], axis=0)
    return lax.dot_general(left, right, (((0,), (0,)), ((), ())), preferred_element_type=F32)


def piece_a(x, k):
    xk = lax.rem(x + k, NX)
    return 0, [(xk * 128, 128), ((xk + NX) * 128, 128)], 0, HALF


def piece_b(y, k):
    yk = lax.rem(y + k, 4)
    return 1, [((yk // 2) * 512, 512)], lax.rem(yk, 2) * QUARTER, QUARTER


def start_rows(first, hid_far, og_far, hid, og, sems):
    half = pl.ds(pl.multiple_of(first, 128), HALF)
    loads = [
        pltpu.make_async_copy(hid_far, hid, sems.at[0]),
        pltpu.make_async_copy(og_far.at[:, half], og, sems.at[1]),
    ]
    for load in loads:
        load.start()
    return loads


def own_kernel(offsets, s, hid_far, og_far, *refs):
    acc_a, acc_b, hid, og, room_a, room_b, row_sems, sems = refs[-8:]
    outs = refs[:-8]
    x, y, c = s[0], s[1], s[2]
    route = 3
    copies = []
    for load in start_rows(c * HALF, hid_far, og_far, hid, og, row_sems):
        load.wait()

    def piece(acc, room, i, where):
        expert, lanes, first, width = where
        acc[...] = tiles_dot(s, hid, og, route, 0, expert, lanes, first, width)

        def more(pair, carry):
            acc[...] += tiles_dot(s, hid, og, route, pair, expert, lanes, first, width)
            return carry

        lax.fori_loop(1, (s[route + BUCKETS * TILES + expert] + 1) // 2, more, 0)
        if i >= 4:
            copies[i - 4].wait()
        slot = (i // 2) % 2
        room[slot] = acc[...].astype(BF16)
        copies.append(pltpu.make_async_copy(room.at[slot], outs[i], sems.at[i]))
        copies[i].start()

    for i, k in enumerate(offsets):
        piece(acc_a, room_a, 2 * i, piece_a(x, k))
        piece(acc_b, room_b, 2 * i + 1, piece_b(y, k))
    for copy in copies[-4:]:
        copy.wait()


def other_kernel(offsets, s, hid_far, og_far, *refs):
    acc_a, acc_b, hid, og, room_a, room_b, row_sems, sems = refs[-8:]
    n = 2 * len(offsets)
    owns, outs = refs[:n], list(refs[n:-8])
    x, y, c = s[0], s[1], s[2]
    route = 3 + ROUTE
    rows = start_rows(c * HALF, hid_far, og_far, hid, og, row_sems)
    loads = []
    for i in range(n):
        room = room_b if i % 2 else room_a
        loads.append(pltpu.make_async_copy(owns[i], room.at[i // 2], sems.at[i]))
        loads[i].start()
    for load in rows:
        load.wait()

    def piece(acc, room, i, where, k):
        expert, lanes, first, width = where
        loads[i].wait()
        acc[...] = room[i // 2].astype(F32)

        def more(pair, carry):
            acc[...] += tiles_dot(s, hid, og, route, pair, expert, lanes, first, width)
            return carry

        lax.fori_loop(0, (s[route + BUCKETS * TILES + expert] + 1) // 2, more, 0)
        parts = 2 if k == 2 else 1
        span = acc.shape[0] // parts
        for part in range(parts):
            outs.pop(0)[...] = acc[part * span : (part + 1) * span].astype(BF16)

    for i, k in enumerate(offsets):
        piece(acc_a, room_a, 2 * i, piece_a(x, k), k)
        piece(acc_b, room_b, 2 * i + 1, piece_b(y, k), k)


SHAPE_A, SHAPE_B = (256, HALF), (512, QUARTER)


def in_far_memory(value):
    return pltpu.with_memory_space_constraint(value, pltpu.HBM)


def gradient_call(kernel, scalars, arrays, outs, out_space, rooms, sems, moved):
    rows = arrays[0].shape[0]
    return pl.pallas_call(
        kernel,
        out_shape=outs,
        in_specs=[smem()] + [pl.BlockSpec(memory_space=pltpu.HBM)] * len(arrays),
        out_specs=[pl.BlockSpec(memory_space=out_space)] * len(outs),
        scratch_shapes=[
            pltpu.VMEM(SHAPE_A, F32),
            pltpu.VMEM(SHAPE_B, F32),
            pltpu.VMEM((rows, arrays[0].shape[1]), BF16),
            pltpu.VMEM((rows, HALF), BF16),
            pltpu.VMEM((rooms,) + SHAPE_A, BF16),
            pltpu.VMEM((rooms,) + SHAPE_B, BF16),
            pltpu.SemaphoreType.DMA((2,)),
            pltpu.SemaphoreType.DMA((sems,)),
        ],
        compiler_params=pltpu.CompilerParams(vmem_limit_bytes=18 * 1024 * 1024),
        cost_estimate=pl.CostEstimate(
            flops=sems * 768 * 256 * HALF, bytes_accessed=moved * 2**20, transcendentals=0
        ),
    )(scalars, *[in_far_memory(array) for array in arrays])


def own_gradients(offsets, scalars, hid, og):
    outs = [pltpu.HBM(SHAPE_A, BF16), pltpu.HBM(SHAPE_B, BF16)] * len(offsets)
    made = gradient_call(
        functools.partial(own_kernel, offsets), scalars, [hid, og], outs, pltpu.HBM, 2, len(outs), 12
    )
    return {k: (made[2 * i], made[2 * i + 1]) for i, k in enumerate(offsets)}


def gradients(offsets, scalars, hid, og, own):
    shapes = []
    for k in offsets:
        if k == 2:
            shapes += [(128, HALF)] * 2 + [(256, QUARTER)] * 2
        else:
            shapes += [SHAPE_A, SHAPE_B]
    made = gradient_call(
        functools.partial(other_kernel, offsets),
        scalars,
        [hid, og] + [part for k in offsets for part in own[k]],
        [near(shape) for shape in shapes],
        pltpu.VMEM,
        len(offsets),
        2 * len(offsets),
        5 + 4 * len(offsets),
    )
    pieces = {}
    for k in offsets:
        take = 2 if k == 2 else 1
        a, made = made[:take], made[take:]
        b, made = made[:take], made[take:]
        pieces[k] = (a, b)
    return pieces


def add32(*terms):
    total = terms[0].astype(F32)
    for term in terms[1:]:
        total = total + term.astype(F32)
    return total


def after(value, *others):
    return lax.optimization_barrier((value, *others))[0]


def merge_kernel(s, *refs):
    for i in range(2):
        left, right, far_lo, far_hi = refs[4 * i : 4 * i + 4]
        left_out, right_out = refs[8 + 2 * i : 10 + 2 * i]
        half = left.shape[0] // 2
        left_out[:half] = add32(left[:half], far_lo[...]).astype(BF16)
        left_out[half:] = left[half:]
        right_out[:half] = right[:half]
        right_out[half:] = add32(right[half:], far_hi[...]).astype(BF16)


def cut_kernel(which, s, own, left, right, *outs):
    x, y = s[4], 2 * s[3] + s[2]
    for k in range(4):
        if which == 0:
            yk = lax.rem(y + k, 4)
            rows = pl.ds(pl.multiple_of((yk // 2) * 128, 128), 128)
            cols = pl.ds(pl.multiple_of(lax.rem(yk, 2) * QUARTER, 128), QUARTER)
        else:
            rows = pl.ds(pl.multiple_of(lax.rem(x + k, NX) * 128, 128), 128)
            cols = slice(None)
        outs[k][...] = add32(own[rows, cols], left[rows, cols], right[rows, cols]).astype(BF16)


def plane_kernel(s, *refs):
    out = refs[8]
    for expert in range(BUCKETS):
        terms = refs[4 * expert : 4 * expert + 4]
        total = add32(*[term[...] for term in terms]).astype(BF16)
        for group in range(4):
            out[2 * group + expert] = total[32 * group : 32 * (group + 1)]


def weight_kernel(s, base, own, back2, back4, back6, out, share):
    group = s[0] // 2
    for k, grad in enumerate((own, back2, back4, back6)):
        rows = pl.ds(pl.multiple_of(lax.rem(group - k + 4, 4) * 32, 32), 32)
        share[rows, :] = grad[...]
        out[rows, :] = (base[rows, :] - learning_rate * grad[...].astype(F32)).astype(BF16)


PLANE = [(dyh, k) for dyh in range(2) for k in range(NX)]


def product_kernel(s, acts, acts_y, acts_z, share, *refs):
    weights, (slots, left, right) = refs[:8], refs[8:]
    z0, c, yl, yh, x = lax.rem(s[0], 2), s[1], s[2], s[3], s[4]
    for i, (dyh, k) in enumerate(PLANE):
        m = (yh ^ dyh) * NX + lax.rem(x - k + NX, NX)
        cols = pl.ds(pl.multiple_of(m * 128, 128), 128)
        right[i * 128 : (i + 1) * 128, :] = weights[i][...]
        for dc in range(2):
            for dyl, rows in ((0, acts), (1, acts_y)):
                j = dyl * 4 + dc
                left[j * 64 : (j + 1) * 64, i * 128 : (i + 1) * 128] = rows[dc, z0, :, cols]
                j = dyl * 4 + 2 + dc
                left[j * 64 : (j + 1) * 64, i * 128 : (i + 1) * 128] = acts_z[dyl, dc, :, cols]
    for dyl in range(2):
        total = jnp.dot(
            left[dyl * 256 : (dyl + 1) * 256, :], right[...], preferred_element_type=F32
        ).astype(BF16)
        for dz in range(2):
            for dc in range(2):
                slot = (c ^ dc) * 4 + (yl ^ dyl) * 2 + (z0 ^ dz)
                first = (dz * 2 + dc) * 64
                slots[slot, 0:64, :] = total[first : first + 64]
                rows = pl.ds(pl.multiple_of((c ^ dc) * 64, 64), 64)
                slots[slot, 64:128, :] = share[rows, :]


def join_kernel(s, momentum, slots, new_momentum, next_out):
    for slot in range(8):
        quarter, e = slot // 2, slot % 2
        cols = slice(quarter * QUARTER, (quarter + 1) * QUARTER)
        next_out[e, :, cols] = slots[slot, 0:64, :]
        new_momentum[e, :, cols] = momentum_decay * momentum[e, :, cols] + slots[
            slot, 64:128, :
        ].astype(F32)


def local(hidden_act, out_grad, tile_list, tile_count, momentum, weight, next_act):
    yh, x, c, yl = [lax.axis_index(name) for name in ("y_hi", "x", "core", "y_lo")]
    z0 = lax.axis_index("z_lo")
    z = lax.axis_index("z_hi") * 2 + z0
    y = yh * 2 + yl
    place = jnp.stack([z, c, yl, yh, x]).astype(jnp.int32)

    core = flip(0, 1, 0)
    route = jnp.concatenate([tile_list.reshape(-1), tile_count.reshape(-1)])
    here = jnp.concatenate([jnp.stack([x, y, c]).astype(jnp.int32), route])
    hid_t = send(hidden_act, core)
    og_t = send(out_grad, core)
    scalars = jnp.concatenate([here, send(route, core)])
    own = own_gradients((2, 1, 3, 0), here, hidden_act, out_grad)

    acts = jnp.stack([next_act, send(next_act, core)])
    acts_y = send(acts, flip(0, 0, 1))

    pieces = gradients((2,), scalars, hid_t, og_t, own)
    (lower_a, upper_a), (lower_b, upper_b) = pieces[2]
    far_b = send(lower_b, shift_y(1)), send(upper_b, shift_y(-1))
    far_a = send(lower_a, shift_x(1)), send(upper_a, shift_x(-1))
    pieces |= gradients((1, 3), scalars, hid_t, og_t, own)
    pieces |= gradients((0,), scalars, hid_t, og_t, own)
    (left_a,), (left_b,) = pieces[1]
    (right_a,), (right_b,) = pieces[3]
    (own_a,), (own_b,) = pieces[0]
    left_a, right_a, left_b, right_b = call(
        merge_kernel,
        place,
        [held(v) for v in (left_a, right_a)]
        + list(far_a)
        + [held(v) for v in (left_b, right_b)]
        + list(far_b),
        [near(SHAPE_A)] * 2 + [near(SHAPE_B)] * 2,
        moved=10 * 2**20,
    )

    def cuts(which, own_part, left, right, shift):
        return call(
            functools.partial(cut_kernel, which),
            place,
            [held(own_part), send(left, shift(1)), send(right, shift(-1))],
            [near((128, QUARTER))] * 4,
            moved=4 * 2**20,
        )

    cut_a = cuts(0, own_a, left_a, right_a, shift_x)
    cut_b = cuts(1, own_b, left_b, right_b, shift_y)
    cut_a, cut_b = lax.optimization_barrier((cut_a, cut_b))

    other_rows = jnp.stack([acts, acts_y])
    other_rows = jnp.where(z0 == 0, other_rows[:, :, 1], other_rows[:, :, 0])
    acts_z = send(other_rows, flip(1, 0, 0))
    base_all = weight.astype(F32) - learning_rate * (momentum_decay * momentum)

    def base_part(which):
        at = (z0, 0, (which * 2 + yl) * QUARTER)
        return lax.dynamic_slice(base_all, at, (1, 64, QUARTER))[0]

    base_own = base_part(c)
    base_t = send(base_part(1 - c), core)
    base = jnp.where(
        c == 0,
        jnp.concatenate([base_own, base_t], axis=0),
        jnp.concatenate([base_t, base_own], axis=0),
    )

    plane_a, plane_b = [cut_a[0]], [cut_b[0]]
    for k in (1, 3, 2):
        plane_a.append(send(cut_a[k], shift_y(k)))
        plane_b.append(send(cut_b[k], shift_x(k)))
    (slots,) = call(
        plane_kernel,
        place,
        plane_a + plane_b,
        [jax.ShapeDtypeStruct((NZ, 32, QUARTER), BF16)],
        moved=3 * 2**20,
    )
    slots = lax.all_to_all(slots, ("z_hi", "z_lo"), 0, 0)
    grad = jnp.sum(slots.astype(F32), axis=0).astype(BF16)
    back = {k: send(grad, shift_z(k)) for k in (4, 2, 6)}
    own_weight, share = call(
        weight_kernel,
        place,
        [base, grad] + [back[k] for k in (2, 4, 6)],
        [near((128, QUARTER))] * 2,
        moved=2**20,
    )
    weights = [own_weight] + [send(own_weight, plane(dyh, k)) for dyh, k in PLANE[1:]]
    (slots,) = call(
        product_kernel,
        place,
        [acts, acts_y, acts_z, held(share)] + weights,
        [jax.ShapeDtypeStruct((8, 128, QUARTER), BF16)],
        [pltpu.VMEM((512, 1024), BF16), pltpu.VMEM((1024, QUARTER), BF16)],
        flops=2 * 512 * 1024 * QUARTER,
        moved=4 * 2**20,
    )
    slots = lax.all_to_all(slots, GROUP, 0, 0)
    new_momentum, next_out = call(
        join_kernel,
        place,
        [momentum, slots],
        [
            jax.ShapeDtypeStruct((BUCKETS, 64, 2 * HALF), F32),
            jax.ShapeDtypeStruct((BUCKETS, 64, 2 * HALF), BF16),
        ],
        moved=6 * 2**20,
    )
    return new_momentum, next_out


def solution(mesh):
    fine = jax.sharding.Mesh(mesh.devices.reshape(2, NX, 2, 2, NZ // 2, 2), AXES)
    node, replica = AXES[:3], AXES[3:]
    in_specs = (
        P(node + replica, None),
        P(node + replica, None),
        P(node, replica, None, None),
        P(node, replica, None),
        P(None, node, None),
        P(None, node, None),
        P(None, node + replica, None),
    )
    out_specs = (P(None, node, None), P(None, node + replica, None))
    return jax.shard_map(local, mesh=fine, in_specs=in_specs, out_specs=out_specs, check_vma=False)
```

```python
import functools

import jax
import jax.numpy as jnp
from jax import lax
from jax.experimental import pallas as pl
from jax.experimental.pallas import tpu as pltpu
from jax.sharding import PartitionSpec as P

BUCKETS = 2
TILE = 128
TILES = 6
AXES = ("y_hi", "x", "core", "y_lo", "z_hi", "z_lo")
GROUP = ("y_hi", "y_lo", "z_lo")
F32 = jnp.float32
BF16 = jnp.bfloat16

momentum_decay = 0.9
learning_rate = 0.01

NX, NY, NZ = 4, 4, 8
FEATURES = 3584
QUARTER = 896
CHUNK = 128
HALF = 512


def flat(yh, x, c, yl, z):
    return ((yh * NX + x) * 2 + c) * 16 + yl * NZ + z


def send(value, move):
    pairs = []
    for yh in range(2):
        for x in range(NX):
            for c in range(2):
                for yl in range(2):
                    for z in range(NZ):
                        here = flat(yh, x, c, yl, z)
                        pairs.append((here, flat(*move(yh, x, c, yl, z))))
    return lax.ppermute(value, AXES, pairs)


def shift_x(k):
    return lambda yh, x, c, yl, z: (yh, (x + k) % NX, c, yl, z)


def shift_y(k):
    def move(yh, x, c, yl, z):
        y = (yh * 2 + yl + k) % NY
        return y // 2, x, c, y % 2, z

    return move


def shift_z(k):
    return lambda yh, x, c, yl, z: (yh, x, c, yl, (z + k) % NZ)


def other_core(yh, x, c, yl, z):
    return yh, x, c ^ 1, yl, z


def other_z(yh, x, c, yl, z):
    return yh, x, c, yl, z ^ 1


def other_y_hi(yh, x, c, yl, z):
    return yh ^ 1, x, c, yl, z


def vmem():
    return pl.BlockSpec(memory_space=pltpu.VMEM)


def smem():
    return pl.BlockSpec(memory_space=pltpu.SMEM)


def near(shape, dtype=BF16):
    return pltpu.VMEM(shape, dtype)


def held(value):
    return pltpu.with_memory_space_constraint(value, pltpu.VMEM)


def in_far_memory(value):
    return pltpu.with_memory_space_constraint(value, pltpu.HBM)


def call(kernel, arrays, outs, scratch=(), flops=0, moved=0, limit=12):
    return pl.pallas_call(
        kernel,
        out_shape=outs,
        in_specs=[vmem()] * len(arrays),
        out_specs=[vmem()] * len(outs),
        scratch_shapes=list(scratch),
        compiler_params=pltpu.CompilerParams(vmem_limit_bytes=limit * 1024 * 1024),
        cost_estimate=pl.CostEstimate(flops=flops, bytes_accessed=moved, transcendentals=0),
    )(*arrays)


def place_x():
    return lax.axis_index("x")


def place_y():
    return lax.axis_index("y_hi") * 2 + lax.axis_index("y_lo")


def place_z():
    return lax.axis_index("z_hi") * 2 + lax.axis_index("z_lo")


def halves_kernel(hid, own, other):
    c = lax.axis_index("core")
    low = lax.broadcasted_iota(jnp.int32, (hid.shape[0], CHUNK), 1) < 64
    for x in range(NX):
        first = hid[:, x * CHUNK : (x + 1) * CHUNK].astype(F32)
        second = hid[:, HALF + x * CHUNK : HALF + (x + 1) * CHUNK].astype(F32)
        core0 = jnp.where(low, first, pltpu.roll(second, 64, 1)).astype(BF16)
        core1 = jnp.where(low, pltpu.roll(first, 64, 1), second).astype(BF16)
        cols = slice(x * CHUNK, (x + 1) * CHUNK)
        own[:, cols] = jnp.where(c == 0, core0, core1)
        other[:, cols] = jnp.where(c == 0, core1, core0)


def grad_kernel(offsets, own, other, with_start, *refs):
    refs = list(refs)

    def take(n):
        out, refs[:n] = refs[:n], []
        return out

    n = len(offsets)
    n_src = own + other
    routes = [take(2) for _ in range(n_src)]
    starts = take(2 * n) if with_start else []
    rows = [take(2) for _ in range(n_src)]
    outs = take(4 if offsets == (2,) and with_start else 2 * n)
    acc_a, acc_b = take(2)
    x, y = place_x(), place_y()

    row_loads = []
    if own:
        og, sems = take(2)
        y_first = lax.rem(y + offsets[0], NY)
        for j in range(NY):
            cols = pl.ds(pl.multiple_of(lax.rem(y_first + j, NY) * QUARTER, 128), QUARTER)
            load = pltpu.make_async_copy(rows[0][1].at[:, cols], og.at[:, cols], sems.at[j])
            load.start()
            row_loads.append(load)
        rows[0][1] = og

    def wait_rows(count):
        for load in row_loads[:count]:
            load.wait()
        del row_loads[:count]

    def pairs(expert, add):
        for (listed, counts), (hid, og) in zip(routes, rows):
            count = counts[0, 0, expert]

            def pair_of_tiles(pair, carry):
                t0 = listed[0, 0, expert, 2 * pair]
                t1 = listed[0, 0, expert, 2 * pair + 1]
                r0 = pl.ds(pl.multiple_of(t0 * TILE, TILE), TILE)
                r1 = pl.ds(pl.multiple_of(t1 * TILE, TILE), TILE)
                both = 2 * pair + 1 < count

                def left(at):
                    h1 = hid[r1, at]
                    h1 = jnp.where(both, h1, jnp.zeros_like(h1))
                    return jnp.concatenate([hid[r0, at], h1], axis=0).T

                def right(cols):
                    return jnp.concatenate([og[r0, cols], og[r1, cols]], axis=0)

                add(left, right)
                return carry

            lax.fori_loop(0, (count + 1) // 2, pair_of_tiles, 0)

    def quarter_at(place):
        return pl.ds(pl.multiple_of(place * QUARTER, 128), QUARTER)

    b_outs, a_outs = outs[len(outs) // 2 :], outs[: len(outs) // 2]
    wait_rows(1)
    for i, k in enumerate(offsets):
        if i == 1:
            wait_rows(NY)
        features = quarter_at(lax.rem(y + k, NY))
        if with_start:
            acc_b[...] = starts[n + i][...].astype(F32)
        else:
            acc_b[...] = jnp.zeros_like(acc_b)

        def add_b(left, right):
            values = right(features)

            def half(h, carry):
                at = pl.ds(pl.multiple_of(h * 256, 256), 256)
                acc_b[at, :] += jnp.dot(left(at), values, preferred_element_type=F32)
                return carry

            lax.fori_loop(0, HALF // 256, half, 0)

        pairs(1, add_b)
        if len(outs) > 2 * n:
            b_outs[0][...] = acc_b[: HALF // 2].astype(BF16)
            b_outs[1][...] = acc_b[HALF // 2 :].astype(BF16)
        else:
            b_outs[i][...] = acc_b[...].astype(BF16)
    wait_rows(NY)
    if with_start:
        for i in range(n):
            acc_a[i * CHUNK : (i + 1) * CHUNK] = starts[i][...].astype(F32)
    else:
        acc_a[...] = jnp.zeros_like(acc_a)
    lanes = [
        pl.ds(pl.multiple_of(lax.rem(x + k, NX) * CHUNK, CHUNK), CHUNK) for k in offsets
    ]

    def add_a(left, right):
        turned = [left(at) for at in lanes]
        turned = turned[0] if n == 1 else jnp.concatenate(turned, axis=0)

        def quarter(q, carry):
            cols = quarter_at(q)
            acc_a[:, cols] += jnp.dot(turned, right(cols), preferred_element_type=F32)
            return carry

        lax.fori_loop(0, NY, quarter, 0)

    pairs(0, add_a)
    if len(outs) > 2 * n:
        a_outs[0][...] = acc_a[: CHUNK // 2].astype(BF16)
        a_outs[1][...] = acc_a[CHUNK // 2 :].astype(BF16)
    else:
        for i in range(n):
            a_outs[i][...] = acc_a[i * CHUNK : (i + 1) * CHUNK].astype(BF16)


SHAPE_A, SHAPE_B = (CHUNK, FEATURES), (HALF, QUARTER)


def gradients(offsets, own=None, other=None, starts=()):
    n = len(offsets)
    if offsets == (2,) and starts:
        outs = [near((CHUNK // 2, FEATURES))] * 2 + [near((HALF // 2, QUARTER))] * 2
    else:
        outs = [near(SHAPE_A)] * n + [near(SHAPE_B)] * n
    sources = [source for source in (own, other) if source]
    scratch = [pltpu.VMEM((n * CHUNK, FEATURES), F32), pltpu.VMEM(SHAPE_B, F32)]
    scalars, rows, specs = [], [], []
    for source in sources:
        scalars += source[:2]
        if source is own:
            rows += [held(source[2]), in_far_memory(source[3])]
            specs += [vmem(), pl.BlockSpec(memory_space=pltpu.HBM)]
            scratch += [pltpu.VMEM(source[3].shape, BF16), pltpu.SemaphoreType.DMA((NY,))]
        else:
            rows += [held(source[2]), held(source[3])]
            specs += [vmem()] * 2
    return pl.pallas_call(
        functools.partial(grad_kernel, offsets, own is not None, other is not None, bool(starts)),
        out_shape=outs,
        in_specs=[smem()] * len(scalars) + [vmem()] * len(starts) + specs,
        out_specs=[vmem()] * len(outs),
        scratch_shapes=scratch,
        compiler_params=pltpu.CompilerParams(vmem_limit_bytes=16 * 1024 * 1024),
        cost_estimate=pl.CostEstimate(
            flops=n * len(sources) * 2 * 768 * CHUNK * FEATURES,
            bytes_accessed=(len(sources) * 6 + n * 4) * 2**20,
            transcendentals=0,
        ),
    )(*scalars, *[held(start) for start in starts], *rows)


def add32(*terms):
    total = terms[0].astype(F32)
    for term in terms[1:]:
        total = total + term.astype(F32)
    return total


def after(value, *others):
    return lax.optimization_barrier((value, *others))[0]


def merge_kernel(*refs):
    for i in range(2):
        left, right, far_lo, far_hi = refs[4 * i : 4 * i + 4]
        left_out, right_out = refs[8 + 2 * i : 10 + 2 * i]
        half = left.shape[0] // 2
        left_out[:half] = add32(left[:half], far_lo[...]).astype(BF16)
        left_out[half:] = left[half:]
        right_out[:half] = right[:half]
        right_out[half:] = add32(right[half:], far_hi[...]).astype(BF16)


def cut_kernel(which, own, left, right, *outs):
    for k in range(4):
        if which == 0:
            yk = lax.rem(place_y() + k, NY)
            rows, cols = slice(None), pl.ds(pl.multiple_of(yk * QUARTER, 128), QUARTER)
        else:
            xk = lax.rem(place_x() + k, NX)
            rows, cols = pl.ds(pl.multiple_of(xk * CHUNK, CHUNK), CHUNK), slice(None)
        outs[k][...] = add32(own[rows, cols], left[rows, cols], right[rows, cols]).astype(BF16)


def plane_kernel(*refs):
    keep, give = refs[8:]
    sums = []
    for expert in range(BUCKETS):
        terms = refs[4 * expert : 4 * expert + 4]
        sums.append(add32(*[term[...] for term in terms]))
    even = lax.axis_index("z_lo") == 0
    keep[...] = jnp.where(even, sums[0], sums[1]).astype(BF16)
    give[...] = jnp.where(even, sums[1], sums[0]).astype(BF16)


def pair_kernel(keep, given, *outs):
    for k in range(4):
        group = lax.rem(lax.axis_index("z_hi") + k, 4)
        rows = pl.ds(pl.multiple_of(group * 32, 32), 32)
        outs[k][...] = add32(keep[rows, :], given[rows, :]).astype(BF16)


def acts_kernel(acts, own, other):
    z0 = lax.axis_index("z_lo")
    low = lax.broadcasted_iota(jnp.int32, (64, CHUNK), 1) < 64
    for out, expert in ((own, z0), (other, 1 - z0)):
        for x in range(NX):
            first = acts[expert, :, x * CHUNK : (x + 1) * CHUNK].astype(F32)
            second = acts[expert, :, HALF + x * CHUNK : HALF + (x + 1) * CHUNK].astype(F32)
            core0 = jnp.where(low, first, pltpu.roll(second, 64, 1)).astype(BF16)
            core1 = jnp.where(low, pltpu.roll(first, 64, 1), second).astype(BF16)
            out[:, x * CHUNK : (x + 1) * CHUNK] = core0
            out[:, HALF + x * CHUNK : HALF + (x + 1) * CHUNK] = core1


def base_kernel(momentum, weight, own, other):
    yh, yl, z0 = lax.axis_index("y_hi"), lax.axis_index("y_lo"), lax.axis_index("z_lo")
    for out, which in ((own, yh), (other, 1 - yh)):
        cols = pl.ds(pl.multiple_of((which * 2 + yl) * QUARTER, 128), QUARTER)
        decayed = momentum_decay * momentum[z0, :, cols]
        out[...] = weight[z0, :, cols].astype(F32) - learning_rate * decayed


def weight_kernel(base_o, base_t, own, back2, back4, back6, out, share):
    yh, group = lax.axis_index("y_hi"), lax.axis_index("z_hi")
    for k, grad in enumerate((own, back2, back4, back6)):
        at = lax.rem(group - k + 4, 4)
        rows = pl.ds(pl.multiple_of(at * 32, 32), 32)
        source = pl.ds(pl.multiple_of(lax.rem(at, 2) * 32, 32), 32)
        base = jnp.where(at // 2 == yh, base_o[source, :], base_t[source, :])
        share[rows, :] = grad[...]
        out[rows, :] = (base - learning_rate * grad[...].astype(F32)).astype(BF16)


def product_kernel(share, *refs):
    acts, weights, (slots, left, right) = refs[:4], refs[4:12], refs[12:]
    z0, c, x, y = lax.axis_index("z_lo"), lax.axis_index("core"), place_x(), place_y()
    for i in range(8):
        dc, k = i // 4, i % 4
        group = (c ^ dc) * NX + lax.rem(x - k + NX, NX)
        cols = pl.ds(pl.multiple_of(group * CHUNK, CHUNK), CHUNK)
        at = slice(i * CHUNK, (i + 1) * CHUNK)
        right[at, :] = weights[i][...]
        for j in range(NY):
            for dz in range(2):
                first = dz * 256 + j * 64
                left[first : first + 64, at] = acts[j][dz, :, cols]
    for dz in range(2):
        total = jnp.dot(
            left[dz * 256 : (dz + 1) * 256, :], right[...], preferred_element_type=F32
        ).astype(BF16)
        for j in range(NY):
            y_to = lax.rem(y - j + NY, NY)
            slot = y_to * 2 + (z0 ^ dz)
            slots[slot, 0:64, :] = total[j * 64 : (j + 1) * 64]
            rows = pl.ds(pl.multiple_of((y_to // 2) * 64, 64), 64)
            slots[slot, 64:128, :] = share[rows, :]


def join_kernel(momentum, slots, new_momentum, next_out):
    for slot in range(8):
        quarter, e = slot // 2, slot % 2
        cols = slice(quarter * QUARTER, (quarter + 1) * QUARTER)
        next_out[e, :, cols] = slots[slot, 0:64, :]
        new_momentum[e, :, cols] = momentum_decay * momentum[e, :, cols] + slots[
            slot, 64:128, :
        ].astype(F32)


def local(hidden_act, out_grad, tile_list, tile_count, momentum, weight, next_act):
    rows = hidden_act.shape[0]

    og_t = send(out_grad, other_core)
    hid_o, hid_x = call(
        halves_kernel, [hidden_act], [near((rows, HALF))] * 2, moved=4 * 2**20, limit=16
    )
    hid_t = send(hid_x, other_core)
    own = (tile_list, tile_count, hid_o, out_grad)
    other = (send(tile_list, other_core), send(tile_count, other_core), hid_t, og_t)
    starts = gradients((2,), own)

    acts, acts_x = call(
        acts_kernel, [next_act], [jax.ShapeDtypeStruct((64, 1024), BF16)] * 2, moved=2**20
    )
    acts_z = send(acts_x, other_z)
    base_o, base_x = call(
        base_kernel, [momentum, weight], [near((64, QUARTER), F32)] * 2, moved=4 * 2**20
    )

    lower_a, upper_a, lower_b, upper_b = gradients((2,), None, other, starts)
    far_b = send(lower_b, shift_y(1)), send(upper_b, shift_y(-1))
    far_a = send(lower_a, shift_x(1)), send(upper_a, shift_x(-1))
    left_a, right_a, left_b, right_b = gradients((1, 3), own, other)
    own_a, own_b = gradients((0,), own, other)
    left_a, right_a, left_b, right_b = call(
        merge_kernel,
        [held(v) for v in (left_a, right_a)]
        + list(far_a)
        + [held(v) for v in (left_b, right_b)]
        + list(far_b),
        [near(SHAPE_A)] * 2 + [near(SHAPE_B)] * 2,
        moved=10 * 2**20,
    )

    def cuts(which, own_part, left, right, shift):
        return call(
            functools.partial(cut_kernel, which),
            [held(own_part), send(left, shift(1)), send(right, shift(-1))],
            [near((CHUNK, QUARTER))] * 4,
            moved=4 * 2**20,
        )

    cut_a = cuts(0, own_a, left_a, right_a, shift_x)
    cut_b = cuts(1, own_b, left_b, right_b, shift_y)
    cut_a, cut_b = lax.optimization_barrier((cut_a, cut_b))

    plane_a, plane_b = [cut_a[0]], [cut_b[0]]
    for k in (1, 3, 2):
        plane_a.append(send(cut_a[k], shift_y(k)))
        plane_b.append(send(cut_b[k], shift_x(k)))
    keep, give = call(
        plane_kernel, plane_a + plane_b, [near((CHUNK, QUARTER))] * 2, moved=3 * 2**20
    )
    given = send(give, other_z)
    pair = jnp.stack([acts, acts_z])
    pair = after(pair, give)
    acts_y = [pair] + [send(pair, shift_y(k)) for k in (1, 2, 3)]
    base_t = send(after(base_x, give), other_y_hi)
    groups = call(pair_kernel, [held(keep), given], [near((32, QUARTER))] * 4, moved=2**20)
    grad = add32(groups[0], *[send(groups[k], shift_z(2 * k)) for k in (2, 1, 3)]).astype(BF16)
    back = {k: send(grad, shift_z(k)) for k in (4, 2, 6)}
    own_weight, share = call(
        weight_kernel,
        [held(base_o), base_t, grad] + [back[k] for k in (2, 4, 6)],
        [near((CHUNK, QUARTER))] * 2,
        moved=2**20,
    )
    weights = [own_weight] + [send(own_weight, shift_x(k)) for k in (1, 2, 3)]
    weights += [send(part, other_core) for part in weights]
    (slots,) = call(
        product_kernel,
        [held(share)] + acts_y + weights,
        [jax.ShapeDtypeStruct((8, 128, QUARTER), BF16)],
        [pltpu.VMEM((512, 1024), BF16), pltpu.VMEM((1024, QUARTER), BF16)],
        flops=2 * 512 * 1024 * QUARTER,
        moved=4 * 2**20,
    )
    slots = lax.all_to_all(slots, GROUP, 0, 0)
    new_momentum, next_out = call(
        join_kernel,
        [momentum, slots],
        [
            jax.ShapeDtypeStruct((BUCKETS, 64, FEATURES), F32),
            jax.ShapeDtypeStruct((BUCKETS, 64, FEATURES), BF16),
        ],
        moved=6 * 2**20,
    )
    return new_momentum, next_out


def solution(mesh):
    fine = jax.sharding.Mesh(mesh.devices.reshape(2, NX, 2, 2, NZ // 2, 2), AXES)
    node, replica = AXES[:3], AXES[3:]
    in_specs = (
        P(node + replica, None),
        P(node + replica, None),
        P(node, replica, None, None),
        P(node, replica, None),
        P(None, node, None),
        P(None, node, None),
        P(None, node + replica, None),
    )
    out_specs = (P(None, node, None), P(None, node + replica, None))
    return jax.shard_map(local, mesh=fine, in_specs=in_specs, out_specs=out_specs, check_vma=False)
```

```python
import functools

import jax
import jax.numpy as jnp
from jax import lax
from jax.experimental import pallas as pl
from jax.experimental.pallas import tpu as pltpu
from jax.sharding import PartitionSpec as P

BUCKETS = 2
TILE = 128
TILES = 6
AXES = ("y_hi", "x", "core", "y_lo", "z_hi", "z_lo")
GROUP = ("y_hi", "y_lo", "z_lo")
F32 = jnp.float32
BF16 = jnp.bfloat16

momentum_decay = 0.9
learning_rate = 0.01

NX, NY, NZ = 4, 4, 8
FEATURES = 3584
QUARTER = 896
CHUNK = 128
HALF = 512


def flat(yh, x, c, yl, z):
    return ((yh * NX + x) * 2 + c) * 16 + yl * NZ + z


def send(value, move):
    pairs = []
    for yh in range(2):
        for x in range(NX):
            for c in range(2):
                for yl in range(2):
                    for z in range(NZ):
                        here = flat(yh, x, c, yl, z)
                        pairs.append((here, flat(*move(yh, x, c, yl, z))))
    return lax.ppermute(value, AXES, pairs)


def shift_x(k):
    return lambda yh, x, c, yl, z: (yh, (x + k) % NX, c, yl, z)


def shift_y(k):
    def move(yh, x, c, yl, z):
        y = (yh * 2 + yl + k) % NY
        return y // 2, x, c, y % 2, z

    return move


def shift_z(k):
    return lambda yh, x, c, yl, z: (yh, x, c, yl, (z + k) % NZ)


def other_core(yh, x, c, yl, z):
    return yh, x, c ^ 1, yl, z


def other_z(yh, x, c, yl, z):
    return yh, x, c, yl, z ^ 1


def other_y_lo(yh, x, c, yl, z):
    return yh, x, c, yl ^ 1, z


def other_y_hi(yh, x, c, yl, z):
    return yh ^ 1, x, c, yl, z


def vmem():
    return pl.BlockSpec(memory_space=pltpu.VMEM)


def smem():
    return pl.BlockSpec(memory_space=pltpu.SMEM)


def near(shape, dtype=BF16):
    return pltpu.VMEM(shape, dtype)


def held(value):
    return pltpu.with_memory_space_constraint(value, pltpu.VMEM)


def in_far_memory(value):
    return pltpu.with_memory_space_constraint(value, pltpu.HBM)


def call(kernel, arrays, outs, scratch=(), flops=0, moved=0, limit=12):
    return pl.pallas_call(
        kernel,
        out_shape=outs,
        in_specs=[vmem()] * len(arrays),
        out_specs=[vmem()] * len(outs),
        scratch_shapes=list(scratch),
        compiler_params=pltpu.CompilerParams(vmem_limit_bytes=limit * 1024 * 1024),
        cost_estimate=pl.CostEstimate(flops=flops, bytes_accessed=moved, transcendentals=0),
    )(*arrays)


def place_x():
    return lax.axis_index("x")


def place_y():
    return lax.axis_index("y_hi") * 2 + lax.axis_index("y_lo")


def place_z():
    return lax.axis_index("z_hi") * 2 + lax.axis_index("z_lo")


def halves_kernel(hid, own, other):
    c = lax.axis_index("core")
    low = lax.broadcasted_iota(jnp.int32, (hid.shape[0], CHUNK), 1) < 64
    for x in range(NX):
        first = hid[:, x * CHUNK : (x + 1) * CHUNK].astype(F32)
        second = hid[:, HALF + x * CHUNK : HALF + (x + 1) * CHUNK].astype(F32)
        core0 = jnp.where(low, first, pltpu.roll(second, 64, 1)).astype(BF16).T
        core1 = jnp.where(low, pltpu.roll(first, 64, 1), second).astype(BF16).T
        units = slice(x * CHUNK, (x + 1) * CHUNK)
        own[units, :] = jnp.where(c == 0, core0, core1)
        other[units, :] = jnp.where(c == 0, core1, core0)


def grad_kernel(offsets, own, other, with_start, *refs):
    refs = list(refs)

    def take(n):
        out, refs[:n] = refs[:n], []
        return out

    n = len(offsets)
    n_src = own + other
    routes = [take(2) for _ in range(n_src)]
    starts = take(2 * n) if with_start else []
    rows = [take(2) for _ in range(n_src)]
    outs = take(4 if offsets == (2,) and with_start else 2 * n)
    x, y = place_x(), place_y()

    (halves,) = take(1)
    row_loads = []
    if own:
        og, sems = take(2)
        y_first = lax.rem(y + offsets[0], NY)
        for j in range(NY):
            cols = pl.ds(pl.multiple_of(lax.rem(y_first + j, NY) * QUARTER, 128), QUARTER)
            load = pltpu.make_async_copy(rows[0][1].at[:, cols], og.at[:, cols], sems.at[j])
            load.start()
            row_loads.append(load)
        rows[0][1] = og

    def wait_rows(count):
        for load in row_loads[:count]:
            load.wait()
        del row_loads[:count]

    def owned(route, expert):
        listed, counts = route
        tile = lax.broadcasted_iota(jnp.int32, (1, TILES * TILE), 1) // TILE
        named = tile < 0
        for i in range(TILES):
            at = jnp.where(i < counts[0, 0, expert], listed[0, 0, expert, i], -1)
            named = jnp.logical_or(named, tile == at)
        return jnp.where(named, 1.0, 0.0).astype(BF16)

    masks = [[owned(route, expert) for expert in range(BUCKETS)] for route in routes]

    def quarter_at(place):
        return pl.ds(pl.multiple_of(place * QUARTER, 128), QUARTER)

    b_outs, a_outs = outs[len(outs) // 2 :], outs[: len(outs) // 2]
    wait_rows(1)
    for i, k in enumerate(offsets):
        if i == 1:
            wait_rows(NY)
        features = quarter_at(lax.rem(y + k, NY))

        def half(h, carry):
            at = pl.ds(pl.multiple_of(h * 256, 256), 256)
            total = starts[n + i][at, :].astype(F32) if with_start else None
            for mask, (hid, og) in zip(masks, rows):
                term = jnp.dot(hid[at, :] * mask[1], og[:, features], preferred_element_type=F32)
                total = term if total is None else total + term
            if len(outs) > 2 * n:
                halves[at, :] = total.astype(BF16)
            else:
                b_outs[i][at, :] = total.astype(BF16)
            return carry

        lax.fori_loop(0, HALF // 256, half, 0)
        if len(outs) > 2 * n:
            b_outs[0][...] = halves[: HALF // 2]
            b_outs[1][...] = halves[HALF // 2 :]
    wait_rows(NY)
    units = [
        pl.ds(pl.multiple_of(lax.rem(x + k, NX) * CHUNK, CHUNK), CHUNK) for k in offsets
    ]

    def quarter(q, carry):
        cols = quarter_at(q)
        total = None
        if with_start:
            total = starts[0][:, cols].astype(F32)
        for mask, (hid, og) in zip(masks, rows):
            left = [hid[at, :] * mask[0] for at in units]
            left = left[0] if n == 1 else jnp.concatenate(left, axis=0)
            term = jnp.dot(left, og[:, cols], preferred_element_type=F32)
            total = term if total is None else total + term
        if len(outs) > 2 * n:
            a_outs[0][:, cols] = total[: CHUNK // 2].astype(BF16)
            a_outs[1][:, cols] = total[CHUNK // 2 :].astype(BF16)
        else:
            for i in range(n):
                a_outs[i][:, cols] = total[i * CHUNK : (i + 1) * CHUNK].astype(BF16)
        return carry

    lax.fori_loop(0, NY, quarter, 0)


SHAPE_A, SHAPE_B = (CHUNK, FEATURES), (HALF, QUARTER)


def gradients(offsets, own=None, other=None, starts=()):
    n = len(offsets)
    if offsets == (2,) and starts:
        outs = [near((CHUNK // 2, FEATURES))] * 2 + [near((HALF // 2, QUARTER))] * 2
    else:
        outs = [near(SHAPE_A)] * n + [near(SHAPE_B)] * n
    sources = [source for source in (own, other) if source]
    scratch = [pltpu.VMEM(SHAPE_B, BF16)]
    scalars, rows, specs = [], [], []
    for source in sources:
        scalars += source[:2]
        if source is own:
            rows += [held(source[2]), in_far_memory(source[3])]
            specs += [vmem(), pl.BlockSpec(memory_space=pltpu.HBM)]
            scratch += [pltpu.VMEM(source[3].shape, BF16), pltpu.SemaphoreType.DMA((NY,))]
        else:
            rows += [held(source[2]), held(source[3])]
            specs += [vmem()] * 2
    return pl.pallas_call(
        functools.partial(grad_kernel, offsets, own is not None, other is not None, bool(starts)),
        out_shape=outs,
        in_specs=[smem()] * len(scalars) + [vmem()] * len(starts) + specs,
        out_specs=[vmem()] * len(outs),
        scratch_shapes=scratch,
        compiler_params=pltpu.CompilerParams(vmem_limit_bytes=16 * 1024 * 1024),
        cost_estimate=pl.CostEstimate(
            flops=n * len(sources) * 2 * 768 * CHUNK * FEATURES,
            bytes_accessed=(len(sources) * 6 + n * 4) * 2**20,
            transcendentals=0,
        ),
    )(*scalars, *[held(start) for start in starts], *rows)


def add32(*terms):
    total = terms[0].astype(F32)
    for term in terms[1:]:
        total = total + term.astype(F32)
    return total


def after(value, *others):
    return lax.optimization_barrier((value, *others))[0]


def merge_kernel(*refs):
    for i in range(2):
        left, right, far_lo, far_hi = refs[4 * i : 4 * i + 4]
        left_out, right_out = refs[8 + 2 * i : 10 + 2 * i]
        half = left.shape[0] // 2
        left_out[:half] = add32(left[:half], far_lo[...]).astype(BF16)
        left_out[half:] = left[half:]
        right_out[:half] = right[:half]
        right_out[half:] = add32(right[half:], far_hi[...]).astype(BF16)


def cut_kernel(which, own, left, right, *outs):
    for k in range(4):
        if which == 0:
            yk = lax.rem(place_y() + k, NY)
            rows, cols = slice(None), pl.ds(pl.multiple_of(yk * QUARTER, 128), QUARTER)
        else:
            xk = lax.rem(place_x() + k, NX)
            rows, cols = pl.ds(pl.multiple_of(xk * CHUNK, CHUNK), CHUNK), slice(None)
        outs[k][...] = add32(own[rows, cols], left[rows, cols], right[rows, cols]).astype(BF16)


def plane_kernel(*refs):
    keep, give = refs[8:]
    sums = []
    for expert in range(BUCKETS):
        terms = refs[4 * expert : 4 * expert + 4]
        sums.append(add32(*[term[...] for term in terms]))
    even = lax.axis_index("z_lo") == 0
    keep[...] = jnp.where(even, sums[0], sums[1]).astype(BF16)
    give[...] = jnp.where(even, sums[1], sums[0]).astype(BF16)


def pair_kernel(keep, given, out):
    out[...] = add32(keep[...], given[...]).astype(BF16)


def acts_kernel(acts, own, other):
    z0 = lax.axis_index("z_lo")
    low = lax.broadcasted_iota(jnp.int32, (64, CHUNK), 1) < 64
    for out, expert in ((own, z0), (other, 1 - z0)):
        for x in range(NX):
            first = acts[expert, :, x * CHUNK : (x + 1) * CHUNK].astype(F32)
            second = acts[expert, :, HALF + x * CHUNK : HALF + (x + 1) * CHUNK].astype(F32)
            core0 = jnp.where(low, first, pltpu.roll(second, 64, 1)).astype(BF16)
            core1 = jnp.where(low, pltpu.roll(first, 64, 1), second).astype(BF16)
            out[:, x * CHUNK : (x + 1) * CHUNK] = core0
            out[:, HALF + x * CHUNK : HALF + (x + 1) * CHUNK] = core1


def base_kernel(momentum, weight, own, other):
    yh, yl, z0 = lax.axis_index("y_hi"), lax.axis_index("y_lo"), lax.axis_index("z_lo")
    for out, which in ((own, yh), (other, 1 - yh)):
        cols = pl.ds(pl.multiple_of((which * 2 + yl) * QUARTER, 128), QUARTER)
        decayed = momentum_decay * momentum[z0, :, cols]
        out[...] = weight[z0, :, cols].astype(F32) - learning_rate * decayed


def weight_kernel(base_o, base_t, own, back1, back2, back3, out, share, terms):
    yh, pair = lax.axis_index("y_hi"), lax.axis_index("z_hi")
    for k, term in enumerate((own, back1, back2, back3)):
        terms[lax.rem(pair - k + 4, 4)] = term[...]
    grad = add32(*[terms[k] for k in range(4)]).astype(BF16)
    share[...] = grad
    step = learning_rate * grad.astype(F32)
    first, second = base_o[...], base_t[...]
    out[0:64, :] = (jnp.where(yh == 0, first, second) - step[0:64]).astype(BF16)
    out[64:128, :] = (jnp.where(yh == 0, second, first) - step[64:128]).astype(BF16)


def product_kernel(share, *refs):
    acts, weights, (slots, left, right) = refs[:2], refs[2:10], refs[10:]
    z0, c, x, y = lax.axis_index("z_lo"), lax.axis_index("core"), place_x(), place_y()
    for i in range(8):
        dc, k = i // 4, i % 4
        group = (c ^ dc) * NX + lax.rem(x - k + NX, NX)
        cols = pl.ds(pl.multiple_of(group * CHUNK, CHUNK), CHUNK)
        at = slice(i * CHUNK, (i + 1) * CHUNK)
        right[at, :] = weights[i][...]
        for j in range(NY):
            for dz in range(2):
                first = dz * 256 + j * 64
                left[first : first + 64, at] = acts[j // 2][j % 2, dz, :, cols]

    def parity(dz, carry):
        rows = pl.ds(pl.multiple_of(dz * 256, 256), 256)
        total = jnp.dot(left[rows, :], right[...], preferred_element_type=F32).astype(BF16)
        for j in range(NY):
            y_to = y ^ j
            slot = y_to * 2 + lax.rem(z0 + dz, 2)
            slots[slot, 0:64, :] = total[j * 64 : (j + 1) * 64]
            share_rows = pl.ds(pl.multiple_of((y_to // 2) * 64, 64), 64)
            slots[slot, 64:128, :] = share[share_rows, :]
        return carry

    lax.fori_loop(0, 2, parity, 0)


def join_kernel(momentum, slots, new_momentum, next_out):
    for slot in range(8):
        quarter, e = slot // 2, slot % 2
        cols = slice(quarter * QUARTER, (quarter + 1) * QUARTER)
        next_out[e, :, cols] = slots[slot, 0:64, :]
        new_momentum[e, :, cols] = momentum_decay * momentum[e, :, cols] + slots[
            slot, 64:128, :
        ].astype(F32)


def local(hidden_act, out_grad, tile_list, tile_count, momentum, weight, next_act):
    rows = hidden_act.shape[0]

    og_t = send(out_grad, other_core)
    hid_o, hid_x = call(
        halves_kernel, [hidden_act], [near((HALF, rows))] * 2, moved=4 * 2**20, limit=16
    )
    hid_t = send(hid_x, other_core)
    own = (tile_list, tile_count, hid_o, out_grad)
    other = (send(tile_list, other_core), send(tile_count, other_core), hid_t, og_t)
    starts = gradients((2,), own)

    acts, acts_x = call(
        acts_kernel, [next_act], [jax.ShapeDtypeStruct((64, 1024), BF16)] * 2, moved=2**20
    )
    acts_z = send(acts_x, other_z)
    base_o, base_x = call(
        base_kernel, [momentum, weight], [near((64, QUARTER), F32)] * 2, moved=4 * 2**20
    )

    lower_a, upper_a, lower_b, upper_b = gradients((2,), None, other, starts)
    far_b = send(lower_b, shift_y(1)), send(upper_b, shift_y(-1))
    far_a = send(lower_a, shift_x(1)), send(upper_a, shift_x(-1))
    left_a, right_a, left_b, right_b = gradients((1, 3), own, other)
    own_a, own_b = gradients((0,), own, other)
    left_a, right_a, left_b, right_b = call(
        merge_kernel,
        [held(v) for v in (left_a, right_a)]
        + list(far_a)
        + [held(v) for v in (left_b, right_b)]
        + list(far_b),
        [near(SHAPE_A)] * 2 + [near(SHAPE_B)] * 2,
        moved=10 * 2**20,
    )

    def cuts(which, own_part, left, right, shift):
        return call(
            functools.partial(cut_kernel, which),
            [held(own_part), send(left, shift(1)), send(right, shift(-1))],
            [near((CHUNK, QUARTER))] * 4,
            moved=4 * 2**20,
        )

    cut_a = cuts(0, own_a, left_a, right_a, shift_x)
    cut_b = cuts(1, own_b, left_b, right_b, shift_y)
    cut_a, cut_b, acts_z, base_x = lax.optimization_barrier((cut_a, cut_b, acts_z, base_x))

    plane_a, plane_b = [cut_a[0]], [cut_b[0]]
    for k in (1, 3, 2):
        plane_a.append(send(cut_a[k], shift_y(k)))
        plane_b.append(send(cut_b[k], shift_x(k)))
    keep, give = call(
        plane_kernel, plane_a + plane_b, [near((CHUNK, QUARTER))] * 2, moved=3 * 2**20
    )
    given = send(give, other_z)
    (pair_sum,) = call(
        pair_kernel, [held(keep), given], [near((CHUNK, QUARTER))], moved=2**20
    )
    others = [send(pair_sum, shift_z(2 * k)) for k in (2, 1, 3)]
    pair = after(jnp.stack([acts, acts_z]), pair_sum)
    four = jnp.stack([pair, send(pair, other_y_lo)])
    acts_y = [four, send(four, other_y_hi)]
    base_t = send(after(base_x, pair_sum), other_y_hi)
    own_weight, share = call(
        weight_kernel,
        [held(base_o), base_t, held(pair_sum)] + [others[i] for i in (1, 0, 2)],
        [near((CHUNK, QUARTER))] * 2,
        [pltpu.VMEM((4, CHUNK, QUARTER), BF16)],
        moved=2**20,
    )
    weights = [own_weight] + [send(own_weight, shift_x(k)) for k in (1, 2, 3)]
    weights += [send(part, other_core) for part in weights]
    (slots,) = call(
        product_kernel,
        [held(share)] + acts_y + weights,
        [jax.ShapeDtypeStruct((8, 128, QUARTER), BF16)],
        [pltpu.VMEM((512, 1024), BF16), pltpu.VMEM((1024, QUARTER), BF16)],
        flops=2 * 512 * 1024 * QUARTER,
        moved=4 * 2**20,
    )
    slots = lax.all_to_all(slots, GROUP, 0, 0)
    new_momentum, next_out = call(
        join_kernel,
        [momentum, slots],
        [
            jax.ShapeDtypeStruct((BUCKETS, 64, FEATURES), F32),
            jax.ShapeDtypeStruct((BUCKETS, 64, FEATURES), BF16),
        ],
        moved=6 * 2**20,
    )
    return new_momentum, next_out


def solution(mesh):
    fine = jax.sharding.Mesh(mesh.devices.reshape(2, NX, 2, 2, NZ // 2, 2), AXES)
    node, replica = AXES[:3], AXES[3:]
    in_specs = (
        P(node + replica, None),
        P(node + replica, None),
        P(node, replica, None, None),
        P(node, replica, None),
        P(None, node, None),
        P(None, node, None),
        P(None, node + replica, None),
    )
    out_specs = (P(None, node, None), P(None, node + replica, None))
    return jax.shard_map(local, mesh=fine, in_specs=in_specs, out_specs=out_specs, check_vma=False)
```

```python
import functools

import jax
import jax.numpy as jnp
from jax import lax
from jax.experimental import pallas as pl
from jax.experimental.pallas import tpu as pltpu
from jax.sharding import PartitionSpec as P

BUCKETS = 2
TILE = 128
TILES = 6
AXES = ("y_hi", "x", "core", "y_lo", "z_hi", "z_lo")
GROUP = ("y_hi", "y_lo", "z_lo")
F32 = jnp.float32
BF16 = jnp.bfloat16

momentum_decay = 0.9
learning_rate = 0.01

NX, NY, NZ = 4, 4, 8
FEATURES = 3584
QUARTER = 896
CHUNK = 128
HALF = 512


def flat(yh, x, c, yl, z):
    return ((yh * NX + x) * 2 + c) * 16 + yl * NZ + z


def send(value, move):
    pairs = []
    for yh in range(2):
        for x in range(NX):
            for c in range(2):
                for yl in range(2):
                    for z in range(NZ):
                        here = flat(yh, x, c, yl, z)
                        pairs.append((here, flat(*move(yh, x, c, yl, z))))
    return lax.ppermute(value, AXES, pairs)


def shift_x(k):
    return lambda yh, x, c, yl, z: (yh, (x + k) % NX, c, yl, z)


def shift_y(k):
    def move(yh, x, c, yl, z):
        y = (yh * 2 + yl + k) % NY
        return y // 2, x, c, y % 2, z

    return move


def shift_z(k):
    return lambda yh, x, c, yl, z: (yh, x, c, yl, (z + k) % NZ)


def other_core(yh, x, c, yl, z):
    return yh, x, c ^ 1, yl, z


def other_z(yh, x, c, yl, z):
    return yh, x, c, yl, z ^ 1


def other_y_lo(yh, x, c, yl, z):
    return yh, x, c, yl ^ 1, z


def other_y_hi(yh, x, c, yl, z):
    return yh ^ 1, x, c, yl, z


def vmem():
    return pl.BlockSpec(memory_space=pltpu.VMEM)


def smem():
    return pl.BlockSpec(memory_space=pltpu.SMEM)


def near(shape, dtype=BF16):
    return pltpu.VMEM(shape, dtype)


def held(value):
    return pltpu.with_memory_space_constraint(value, pltpu.VMEM)


def in_far_memory(value):
    return pltpu.with_memory_space_constraint(value, pltpu.HBM)


def call(kernel, arrays, outs, scratch=(), flops=0, moved=0, limit=12):
    return pl.pallas_call(
        kernel,
        out_shape=outs,
        in_specs=[vmem()] * len(arrays),
        out_specs=[vmem()] * len(outs),
        scratch_shapes=list(scratch),
        compiler_params=pltpu.CompilerParams(vmem_limit_bytes=limit * 1024 * 1024),
        cost_estimate=pl.CostEstimate(flops=flops, bytes_accessed=moved, transcendentals=0),
    )(*arrays)


def place_x():
    return lax.axis_index("x")


def place_y():
    return lax.axis_index("y_hi") * 2 + lax.axis_index("y_lo")


def place_z():
    return lax.axis_index("z_hi") * 2 + lax.axis_index("z_lo")


def halves_kernel(hid, own, other):
    c = lax.axis_index("core")
    low = lax.broadcasted_iota(jnp.int32, (hid.shape[0], CHUNK), 1) < 64
    for x in range(NX):
        first = hid[:, x * CHUNK : (x + 1) * CHUNK].astype(F32)
        second = hid[:, HALF + x * CHUNK : HALF + (x + 1) * CHUNK].astype(F32)
        core0 = jnp.where(low, first, pltpu.roll(second, 64, 1)).astype(BF16).T
        core1 = jnp.where(low, pltpu.roll(first, 64, 1), second).astype(BF16).T
        units = slice(x * CHUNK, (x + 1) * CHUNK)
        own[units, :] = jnp.where(c == 0, core0, core1)
        other[units, :] = jnp.where(c == 0, core1, core0)


def grad_kernel(offsets, own, other, with_start, *refs):
    refs = list(refs)

    def take(n):
        out, refs[:n] = refs[:n], []
        return out

    n = len(offsets)
    n_src = own + other
    routes = [take(2) for _ in range(n_src)]
    starts = take(2 * n) if with_start else []
    rows = [take(2) for _ in range(n_src)]
    outs = take(4 if offsets == (2,) and with_start else 2 * n)
    x, y = place_x(), place_y()

    (halves,) = take(1)
    row_loads = []
    if own:
        og, sems = take(2)
        y_first = lax.rem(y + offsets[0], NY)
        for j in range(NY):
            cols = pl.ds(pl.multiple_of(lax.rem(y_first + j, NY) * QUARTER, 128), QUARTER)
            load = pltpu.make_async_copy(rows[0][1].at[:, cols], og.at[:, cols], sems.at[j])
            load.start()
            row_loads.append(load)
        rows[0][1] = og

    def wait_rows(count):
        for load in row_loads[:count]:
            load.wait()
        del row_loads[:count]

    def owned(route, expert):
        listed, counts = route
        tile = lax.broadcasted_iota(jnp.int32, (1, TILES * TILE), 1) // TILE
        named = tile < 0
        for i in range(TILES):
            at = jnp.where(i < counts[0, 0, expert], listed[0, 0, expert, i], -1)
            named = jnp.logical_or(named, tile == at)
        return jnp.where(named, 1.0, 0.0).astype(BF16)

    masks = [[owned(route, expert) for expert in range(BUCKETS)] for route in routes]

    def quarter_at(place):
        return pl.ds(pl.multiple_of(place * QUARTER, 128), QUARTER)

    b_outs, a_outs = outs[len(outs) // 2 :], outs[: len(outs) // 2]
    wait_rows(1)
    for i, k in enumerate(offsets):
        if i == 1:
            wait_rows(NY)
        features = quarter_at(lax.rem(y + k, NY))

        def half(h, carry):
            at = pl.ds(pl.multiple_of(h * 256, 256), 256)
            total = starts[n + i][at, :].astype(F32) if with_start else None
            for mask, (hid, og) in zip(masks, rows):
                term = jnp.dot(hid[at, :] * mask[1], og[:, features], preferred_element_type=F32)
                total = term if total is None else total + term
            if len(outs) > 2 * n:
                halves[at, :] = total.astype(BF16)
            else:
                b_outs[i][at, :] = total.astype(BF16)
            return carry

        lax.fori_loop(0, HALF // 256, half, 0)
        if len(outs) > 2 * n:
            b_outs[0][...] = halves[: HALF // 2]
            b_outs[1][...] = halves[HALF // 2 :]
    wait_rows(NY)
    units = [
        pl.ds(pl.multiple_of(lax.rem(x + k, NX) * CHUNK, CHUNK), CHUNK) for k in offsets
    ]

    def quarter(q, carry):
        cols = quarter_at(q)
        total = None
        if with_start:
            total = starts[0][:, cols].astype(F32)
        for mask, (hid, og) in zip(masks, rows):
            left = [hid[at, :] * mask[0] for at in units]
            left = left[0] if n == 1 else jnp.concatenate(left, axis=0)
            term = jnp.dot(left, og[:, cols], preferred_element_type=F32)
            total = term if total is None else total + term
        if len(outs) > 2 * n:
            a_outs[0][:, cols] = total[: CHUNK // 2].astype(BF16)
            a_outs[1][:, cols] = total[CHUNK // 2 :].astype(BF16)
        else:
            for i in range(n):
                a_outs[i][:, cols] = total[i * CHUNK : (i + 1) * CHUNK].astype(BF16)
        return carry

    lax.fori_loop(0, NY, quarter, 0)


SHAPE_A, SHAPE_B = (CHUNK, FEATURES), (HALF, QUARTER)


def gradients(offsets, own=None, other=None, starts=()):
    n = len(offsets)
    if offsets == (2,) and starts:
        outs = [near((CHUNK // 2, FEATURES))] * 2 + [near((HALF // 2, QUARTER))] * 2
    else:
        outs = [near(SHAPE_A)] * n + [near(SHAPE_B)] * n
    sources = [source for source in (own, other) if source]
    scratch = [pltpu.VMEM(SHAPE_B, BF16)]
    scalars, rows, specs = [], [], []
    for source in sources:
        scalars += source[:2]
        if source is own:
            rows += [held(source[2]), in_far_memory(source[3])]
            specs += [vmem(), pl.BlockSpec(memory_space=pltpu.HBM)]
            scratch += [pltpu.VMEM(source[3].shape, BF16), pltpu.SemaphoreType.DMA((NY,))]
        else:
            rows += [held(source[2]), held(source[3])]
            specs += [vmem()] * 2
    return pl.pallas_call(
        functools.partial(grad_kernel, offsets, own is not None, other is not None, bool(starts)),
        out_shape=outs,
        in_specs=[smem()] * len(scalars) + [vmem()] * len(starts) + specs,
        out_specs=[vmem()] * len(outs),
        scratch_shapes=scratch,
        compiler_params=pltpu.CompilerParams(vmem_limit_bytes=16 * 1024 * 1024),
        cost_estimate=pl.CostEstimate(
            flops=n * len(sources) * 2 * 768 * CHUNK * FEATURES,
            bytes_accessed=(len(sources) * 6 + n * 4) * 2**20,
            transcendentals=0,
        ),
    )(*scalars, *[held(start) for start in starts], *rows)


def add32(*terms):
    total = terms[0].astype(F32)
    for term in terms[1:]:
        total = total + term.astype(F32)
    return total


def after(value, *others):
    return lax.optimization_barrier((value, *others))[0]


def merge_kernel(*refs):
    for i in range(2):
        left, right, far_lo, far_hi = refs[4 * i : 4 * i + 4]
        left_out, right_out = refs[8 + 2 * i : 10 + 2 * i]
        half = left.shape[0] // 2
        left_out[:half] = add32(left[:half], far_lo[...]).astype(BF16)
        left_out[half:] = left[half:]
        right_out[:half] = right[:half]
        right_out[half:] = add32(right[half:], far_hi[...]).astype(BF16)


def cut_kernel(which, own, left, right, *outs):
    for k in range(4):
        if which == 0:
            yk = lax.rem(place_y() + k, NY)
            rows, cols = slice(None), pl.ds(pl.multiple_of(yk * QUARTER, 128), QUARTER)
        else:
            xk = lax.rem(place_x() + k, NX)
            rows, cols = pl.ds(pl.multiple_of(xk * CHUNK, CHUNK), CHUNK), slice(None)
        outs[k][...] = add32(own[rows, cols], left[rows, cols], right[rows, cols]).astype(BF16)


def plane_kernel(*refs):
    keep, give = refs[8:]
    sums = []
    for expert in range(BUCKETS):
        terms = refs[4 * expert : 4 * expert + 4]
        sums.append(add32(*[term[...] for term in terms]))
    even = lax.axis_index("z_lo") == 0
    keep[...] = jnp.where(even, sums[0], sums[1]).astype(BF16)
    give[...] = jnp.where(even, sums[1], sums[0]).astype(BF16)


def pair_kernel(keep, given, out):
    out[...] = add32(keep[...], given[...]).astype(BF16)


def acts_kernel(acts, own, other):
    z0 = lax.axis_index("z_lo")
    low = lax.broadcasted_iota(jnp.int32, (64, CHUNK), 1) < 64
    for out, expert in ((own, z0), (other, 1 - z0)):
        for x in range(NX):
            first = acts[expert, :, x * CHUNK : (x + 1) * CHUNK].astype(F32)
            second = acts[expert, :, HALF + x * CHUNK : HALF + (x + 1) * CHUNK].astype(F32)
            core0 = jnp.where(low, first, pltpu.roll(second, 64, 1)).astype(BF16)
            core1 = jnp.where(low, pltpu.roll(first, 64, 1), second).astype(BF16)
            out[:, x * CHUNK : (x + 1) * CHUNK] = core0
            out[:, HALF + x * CHUNK : HALF + (x + 1) * CHUNK] = core1


def base_kernel(momentum, weight, own, other):
    yh, yl, z0 = lax.axis_index("y_hi"), lax.axis_index("y_lo"), lax.axis_index("z_lo")
    for out, which in ((own, yh), (other, 1 - yh)):
        cols = pl.ds(pl.multiple_of((which * 2 + yl) * QUARTER, 128), QUARTER)
        decayed = momentum_decay * momentum[z0, :, cols]
        out[...] = weight[z0, :, cols].astype(F32) - learning_rate * decayed


def weight_kernel(base_o, base_t, own, back1, back2, back3, out, share, terms):
    yh, pair = lax.axis_index("y_hi"), lax.axis_index("z_hi")
    for k, term in enumerate((own, back1, back2, back3)):
        terms[lax.rem(pair - k + 4, 4)] = term[...]
    grad = add32(*[terms[k] for k in range(4)]).astype(BF16)
    share[...] = grad
    step = learning_rate * grad.astype(F32)
    first, second = base_o[...], base_t[...]
    out[0:64, :] = (jnp.where(yh == 0, first, second) - step[0:64]).astype(BF16)
    out[64:128, :] = (jnp.where(yh == 0, second, first) - step[64:128]).astype(BF16)


def product_kernel(share, *refs):
    acts, weights, (slots, left, right) = refs[:2], refs[2:10], refs[10:]
    z0, c, x, y = lax.axis_index("z_lo"), lax.axis_index("core"), place_x(), place_y()
    for i in range(8):
        dc, k = i // 4, i % 4
        group = (c ^ dc) * NX + lax.rem(x - k + NX, NX)
        cols = pl.ds(pl.multiple_of(group * CHUNK, CHUNK), CHUNK)
        at = slice(i * CHUNK, (i + 1) * CHUNK)
        right[at, :] = weights[i][...]
        for j in range(NY):
            for dz in range(2):
                first = dz * 256 + j * 64
                left[first : first + 64, at] = acts[j // 2][j % 2, dz, :, cols]

    def parity(dz, carry):
        rows = pl.ds(pl.multiple_of(dz * 256, 256), 256)
        total = jnp.dot(left[rows, :], right[...], preferred_element_type=F32).astype(BF16)
        for j in range(NY):
            y_to = y ^ j
            slot = y_to * 2 + lax.rem(z0 + dz, 2)
            slots[slot, 0:64, :] = total[j * 64 : (j + 1) * 64]
            share_rows = pl.ds(pl.multiple_of((y_to // 2) * 64, 64), 64)
            slots[slot, 64:128, :] = share[share_rows, :]
        return carry

    lax.fori_loop(0, 2, parity, 0)


def join_kernel(momentum, slots, new_momentum, next_out):
    for slot in range(8):
        quarter, e = slot // 2, slot % 2
        cols = slice(quarter * QUARTER, (quarter + 1) * QUARTER)
        next_out[e, :, cols] = slots[slot, 0:64, :]
        new_momentum[e, :, cols] = momentum_decay * momentum[e, :, cols] + slots[
            slot, 64:128, :
        ].astype(F32)


def local(hidden_act, out_grad, tile_list, tile_count, momentum, weight, next_act):
    rows = hidden_act.shape[0]

    og_t = send(out_grad, other_core)
    hid_o, hid_x = call(
        halves_kernel, [hidden_act], [near((HALF, rows))] * 2, moved=4 * 2**20, limit=16
    )
    hid_t = send(hid_x, other_core)
    own = (tile_list, tile_count, hid_o, out_grad)
    other = (send(tile_list, other_core), send(tile_count, other_core), hid_t, og_t)
    starts = gradients((2,), own)

    acts, acts_x = call(
        acts_kernel, [next_act], [jax.ShapeDtypeStruct((64, 1024), BF16)] * 2, moved=2**20
    )
    acts_z = send(acts_x, other_z)
    base_o, base_x = call(
        base_kernel, [momentum, weight], [near((64, QUARTER), F32)] * 2, moved=4 * 2**20
    )

    lower_a, upper_a, lower_b, upper_b = gradients((2,), None, other, starts)
    far_b = send(lower_b, shift_y(1)), send(upper_b, shift_y(-1))
    far_a = send(lower_a, shift_x(1)), send(upper_a, shift_x(-1))
    left_a, right_a, left_b, right_b = gradients((1, 3), own, other)
    own_a, own_b = gradients((0,), own, other)
    left_a, right_a, left_b, right_b = call(
        merge_kernel,
        [held(v) for v in (left_a, right_a)]
        + list(far_a)
        + [held(v) for v in (left_b, right_b)]
        + list(far_b),
        [near(SHAPE_A)] * 2 + [near(SHAPE_B)] * 2,
        moved=10 * 2**20,
    )

    def cuts(which, own_part, left, right, shift):
        return call(
            functools.partial(cut_kernel, which),
            [held(own_part), send(left, shift(1)), send(right, shift(-1))],
            [near((CHUNK, QUARTER))] * 4,
            moved=4 * 2**20,
        )

    cut_a = cuts(0, own_a, left_a, right_a, shift_x)
    cut_b = cuts(1, own_b, left_b, right_b, shift_y)
    cut_a, cut_b, acts_z, base_x = lax.optimization_barrier((cut_a, cut_b, acts_z, base_x))

    plane_a, plane_b = [cut_a[0]], [cut_b[0]]
    plane_a += [send(cut_a[k], shift_y(k)) for k in (1, 2, 3)]
    plane_b += [send(cut_b[k], shift_x(k)) for k in (2, 1, 3)]
    keep, give = call(
        plane_kernel, plane_a + plane_b, [near((CHUNK, QUARTER))] * 2, moved=3 * 2**20
    )
    given = send(give, other_z)
    (pair_sum,) = call(
        pair_kernel, [held(keep), given], [near((CHUNK, QUARTER))], moved=2**20
    )
    others = [send(pair_sum, shift_z(2 * k)) for k in (2, 1, 3)]
    pair = after(jnp.stack([acts, acts_z]), pair_sum)
    four = jnp.stack([pair, send(pair, other_y_lo)])
    acts_y = [four, send(four, other_y_hi)]
    base_t = send(after(base_x, pair_sum), other_y_hi)
    own_weight, share = call(
        weight_kernel,
        [held(base_o), base_t, held(pair_sum)] + [others[i] for i in (1, 0, 2)],
        [near((CHUNK, QUARTER))] * 2,
        [pltpu.VMEM((4, CHUNK, QUARTER), BF16)],
        moved=2**20,
    )
    weights = [own_weight] + [send(own_weight, shift_x(k)) for k in (1, 2, 3)]
    weights += [send(part, other_core) for part in weights]
    (slots,) = call(
        product_kernel,
        [held(share)] + acts_y + weights,
        [jax.ShapeDtypeStruct((8, 128, QUARTER), BF16)],
        [pltpu.VMEM((512, 1024), BF16), pltpu.VMEM((1024, QUARTER), BF16)],
        flops=2 * 512 * 1024 * QUARTER,
        moved=4 * 2**20,
    )
    slots = lax.all_to_all(slots, GROUP, 0, 0)
    new_momentum, next_out = call(
        join_kernel,
        [momentum, slots],
        [
            jax.ShapeDtypeStruct((BUCKETS, 64, FEATURES), F32),
            jax.ShapeDtypeStruct((BUCKETS, 64, FEATURES), BF16),
        ],
        moved=6 * 2**20,
    )
    return new_momentum, next_out


def solution(mesh):
    fine = jax.sharding.Mesh(mesh.devices.reshape(2, NX, 2, 2, NZ // 2, 2), AXES)
    node, replica = AXES[:3], AXES[3:]
    in_specs = (
        P(node + replica, None),
        P(node + replica, None),
        P(node, replica, None, None),
        P(node, replica, None),
        P(None, node, None),
        P(None, node, None),
        P(None, node + replica, None),
    )
    out_specs = (P(None, node, None), P(None, node + replica, None))
    return jax.shard_map(local, mesh=fine, in_specs=in_specs, out_specs=out_specs, check_vma=False)
```
